32 devices in a mesh: row: 4 (over y, x), col: 4 (over z), layer: 2 (over core).
Axes of the slice: x: 2, y: 2, z: 4, core: 2. Of those that a mesh axis runs over, the one named last changes fastest.
Arguments:
- similarity: bfloat16 [6144, 6144], P('row', ('col', 'layer')), may hold values from 0.049804688 to 1
- block_mask: int32 [48, 48], P('row', ('col', 'layer')), may hold values from 0 to 1, as said below
Outputs:
- normalized: float32 [6144, 6144], P('row', ('col', 'layer'))
The draws below stay inside these ranges and needn't reach their ends.
Inputs may be any that keep to these rules, and one draw needn't show every extreme that they name: Entries are 0 or 1; every diagonal block is 1; each device's share of block_mask holds at most 18 ones, and some device's share holds exactly 18.
All inputs are finite; a program needn't handle non-finite values.
Results may differ from the reference program's by a relative error of at most 0.0003.
Values may be sent and summed in bfloat16 or wider, within the bound.
No kernel may reach another device: no remote copies, remote signals or barrier semaphores. Data moves between devices by JAX's collectives and lax.ppermute only.
A program may use at most 256 MiB of HBM per device.

```python
import jax
import jax.numpy as jnp

BLK = 128
NB_DEV = 6
NBLK = 48
N = 6144
MAXNZ = 18
N_ROW = 4


def draw_block_mask(key, part):
    key = jax.random.fold_in(key, 7)
    first_key, second_key, third_key = jax.random.split(key, 3)
    tile_rows = NBLK // N_ROW
    tile_cols = NBLK // NB_DEV
    tile_size = tile_rows * NB_DEV
    tile_keys = jax.random.split(first_key, N_ROW * tile_cols)
    ranks = jax.vmap(lambda k: jax.random.permutation(k, tile_size))(tile_keys)
    ranks = ranks.reshape(N_ROW, tile_cols, tile_size).astype(jnp.int32)
    diagonal = jnp.arange(NBLK)[:, None] == jnp.arange(NBLK)[None, :]
    diag_tiles = diagonal.reshape(N_ROW, tile_rows, tile_cols, NB_DEV).transpose(0, 2, 1, 3).reshape(N_ROW, tile_cols, tile_size)
    shifted = jnp.where(diag_tiles, ranks - tile_size, ranks)
    order = jnp.argsort(jnp.argsort(shifted, axis=-1, stable=True), axis=-1, stable=True).astype(jnp.int32)
    lowest = jnp.where(jnp.any(diag_tiles, axis=-1), NB_DEV, 1).astype(jnp.int32)
    spread = jax.random.randint(second_key, (N_ROW, tile_cols), 0, 4096)
    counts = lowest + spread % (MAXNZ + 1 - lowest)
    special = jax.random.randint(third_key, (), 0, N_ROW * tile_cols)
    places = jnp.arange(N_ROW * tile_cols).reshape(N_ROW, tile_cols)
    counts = jnp.where(places == special, MAXNZ, counts)
    chosen = order < counts[:, :, None]
    back = chosen.reshape(N_ROW, tile_cols, tile_rows, NB_DEV).transpose(0, 2, 1, 3).reshape(NBLK, NBLK)
    return jnp.where(back, 1, 0).astype(jnp.int32)


def steps_of(key, extent, cuts, low, top_value):
    def one(axis_at, shards_of):
        draws = jax.random.uniform(jax.random.fold_in(jax.random.fold_in(key, 6), axis_at), (shards_of,), jnp.float32, low / len(cuts), top_value / len(cuts))
        return jnp.repeat(jnp.exp(draws), extent[axis_at] // shards_of).reshape((-1,) + (1,) * (len(extent) - axis_at - 1))

    loudness = one(*cuts[0])
    for cut in cuts[1:]:
        loudness = loudness * one(*cut)
    return loudness


def setup_inputs(seed: int = 0) -> dict:
    splits = jax.random.split(jax.random.key(seed), 3)
    similarity = jnp.clip(0.049804688 + 0.9501953 * jax.random.uniform(splits[0], (N, N), jnp.float32) ** steps_of(splits[0], (N, N), ((0, 4), (1, 8)), -0.2, 0.2), 0.049804688, 1.0).astype(jnp.bfloat16)
    block_mask = draw_block_mask(jax.random.fold_in(splits[2], 71), 0)
    return {"similarity": similarity, "block_mask": block_mask}


def reference(similarity, block_mask):
    expanded = jnp.repeat(jnp.repeat(block_mask, BLK, 0), BLK, 1).astype(jnp.bfloat16)
    masked = similarity * expanded
    product = jnp.dot(masked, masked, preferred_element_type=jnp.float32)
    inflated = product * product
    totals = jnp.sum(inflated, axis=0)
    return (NBLK * BLK) * inflated / totals
```

```python
import functools

import jax
import jax.numpy as jnp
from jax import lax
from jax.experimental import pallas as pl
from jax.experimental.pallas import tpu as pltpu
from jax.sharding import PartitionSpec as P

BLK = 128
SLOTS = 18
SHARE = SLOTS * BLK
HEAD = 16
ROWS = HEAD + SHARE
UNROLL = 4
MIB = 1024 * 1024

SMEM = pl.BlockSpec(memory_space=pltpu.SMEM)
VMEM = pl.BlockSpec(memory_space=pltpu.VMEM)
ANY = pl.BlockSpec(memory_space=pl.ANY)
SMALL = pl.CostEstimate(flops=10**8, bytes_accessed=10**6, transcendentals=0)


def compact_kernel(mask_ref, sim_ref, out_ref, places, sems):
    nb_cols, nb_rows = mask_ref.shape

    def block_copy(slot, i, k):
        return pltpu.make_async_copy(
            sim_ref.at[pl.ds(pl.multiple_of(i * BLK, BLK), BLK), pl.ds(k * BLK, BLK)],
            out_ref.at[pl.ds(pl.multiple_of(HEAD + slot * BLK, HEAD), BLK), :],
            sems.at[slot],
        )

    def scan(i, count):
        for k in range(nb_cols):
            here = mask_ref[k, i]

            @pl.when(here != 0)
            def _():
                block_copy(count, i, k).start()
                places[count] = i * 8 + k

            count = count + here
        return count

    for slot in range(SLOTS):
        places[slot] = 0
    count = lax.fori_loop(0, nb_rows, scan, jnp.int32(0))
    lane = lax.broadcasted_iota(jnp.int32, (HEAD, BLK), 1)
    header = jnp.where(lane == SLOTS, count, 0)
    for slot in range(SLOTS):
        header = jnp.where(lane == slot, places[slot], header)
    out_ref[0:HEAD, :] = header.astype(jnp.float32).astype(out_ref.dtype)

    def wait(slot, carry):
        block_copy(slot, 0, 0).wait()
        return carry

    lax.fori_loop(0, count, wait, 0)


def compact(mask, similarity):
    return pl.pallas_call(
        compact_kernel,
        out_shape=jax.ShapeDtypeStruct((ROWS, BLK), similarity.dtype),
        in_specs=[SMEM, ANY],
        out_specs=VMEM,
        scratch_shapes=[pltpu.SMEM((SLOTS,), jnp.int32), pltpu.SemaphoreType.DMA((SLOTS,))],
        cost_estimate=pl.CostEstimate(flops=0, bytes_accessed=2 * SHARE * BLK * 2, transcendentals=0),
        name="compact",
    )(mask, similarity)


def multiply_pairs(todo, share, x_ref, y_blocks, acc, sums, x_base=0):
    def multiply(step, carry):
        terms = []
        for u in range(UNROLL):
            packed = todo[share, 1 + step * UNROLL + u]
            x = x_base + HEAD + lax.shift_right_logical(packed, 22) * BLK
            y = jnp.bitwise_and(lax.shift_right_logical(packed, 7), 4095) * HEAD
            x_block = x_ref[pl.ds(pl.multiple_of(x, HEAD), BLK), :]
            y_block = y_blocks[pl.ds(pl.multiple_of(y, HEAD), BLK), :]
            terms.append((packed, jnp.dot(x_block, y_block, preferred_element_type=jnp.float32)))
        for packed, term in terms:
            at = jnp.bitwise_and(packed, 127)
            j = jnp.bitwise_and(lax.shift_right_logical(packed, 19), 7)
            old = acc[at]
            new = old + term
            acc[at] = new
            sums[j] += jnp.sum((term * (old + new)).reshape(BLK // 8, 8, BLK), axis=0)
        return carry

    n_steps = lax.shift_right_logical(todo[share, 0] + UNROLL - 1, UNROLL.bit_length() - 1)
    lax.fori_loop(0, n_steps, multiply, 0)


def list_pairs(todo, share, places, at, n_slots, first_inner, slots_of, n_of, nb_rows, nb_cols):
    def slot_pairs(slot, count):
        place = places[at, slot]
        k = first_inner + jnp.bitwise_and(place, 7)
        packed = (slot << 22) + lax.shift_right_logical(place, 3) * nb_cols

        def pair(n, count):
            todo[share, 1 + count] = packed + slots_of[k * 8 + n]
            return count + 1

        return lax.fori_loop(0, n_of[k], pair, count)

    count = lax.fori_loop(0, n_slots, slot_pairs, jnp.int32(0))
    for u in range(UNROLL):
        todo[share, 1 + count + u] = (nb_cols << 19) + nb_rows * nb_cols
    todo[share, 0] = count


def clear_blocks(ref):
    def clear(at, carry):
        ref[at] = jnp.zeros(ref.shape[1:], ref.dtype)
        return carry

    lax.fori_loop(0, ref.shape[0], clear, 0)


def read_headers(headers, heads, places, sem):
    for at, header in enumerate(headers):
        heads[at : at + 1, :] = header.astype(jnp.float32)[0:1, :].astype(jnp.int32)
    copy = pltpu.make_async_copy(heads, places, sem)
    copy.start()
    return copy


def inner_of(n_col, nb_rows, nb_cols, tile, layer):
    valid = jnp.logical_and(tile >= 0, tile < n_col)
    return valid, jnp.where(valid, tile, 0) * nb_rows + layer * nb_cols


def tile_rows(y_blocks, tile, rows=ROWS):
    return y_blocks.at[pl.ds(pl.multiple_of(tile * ROWS, HEAD), rows), :]


def column_headers(y_blocks, r, n_row):
    return [tile_rows(y_blocks, jnp.bitwise_xor(r, m), HEAD)[...] for m in range(n_row)]


def list_column(slots_of, n_of, places, sources, r, nb_rows):
    def no_slots(k, carry):
        n_of[k] = 0
        return carry

    lax.fori_loop(0, n_of.shape[0], no_slots, 0)
    for at, m in sources:
        tile = jnp.bitwise_xor(r, m)
        first = tile * (ROWS // HEAD) + 1

        def put(slot, carry):
            place = places[at, slot]
            k = tile * nb_rows + lax.shift_right_logical(place, 3)
            n = n_of[k]
            j = jnp.bitwise_and(place, 7)
            slots_of[k * 8 + n] = (j << 19) + ((first + slot * (BLK // HEAD)) << 7) + j
            n_of[k] = n + 1
            return carry

        lax.fori_loop(0, places[at, SLOTS], put, 0)


def chain_tile(c, step, odd):
    forward = 1 - 2 * jnp.bitwise_and(c, 1)
    return c - step * forward if odd else c + step * forward


def first_kernel(near, n_col, nb_rows, nb_cols, place_ref, *refs):
    y_refs, refs = refs[: len(near)], refs[len(near) :]
    x_refs, refs = refs[:3], refs[3:]
    acc, sums, y_blocks, slots_of, n_of, heads, places, todo, y_sems, smem_sem = refs
    r, c, l = place_ref[0], place_ref[1], place_ref[2]
    copies = []
    for at, (m, y_ref) in enumerate(zip(near, y_refs)):
        copies.append(pltpu.make_async_copy(y_ref, tile_rows(y_blocks, jnp.bitwise_xor(r, m)), y_sems.at[at]))
        copies[-1].start()
    clear_blocks(acc)
    clear_blocks(sums)
    for copy in copies:
        copy.wait()
    headers = [tile_rows(y_blocks, jnp.bitwise_xor(r, m), HEAD)[...] for m in near]
    read_headers(headers + [ref[0:HEAD, :] for ref in x_refs], heads, places, smem_sem).wait()
    list_column(slots_of, n_of, places, list(enumerate(near)), r, nb_rows)
    shares = [(c, l, 0, y_blocks, r * ROWS), (c, 1 - l, len(near), x_refs[0], 0)]
    shares.append((chain_tile(c, 1, True), l, len(near) + 1, x_refs[1], 0))
    shares.append((chain_tile(c, 1, False), l, len(near) + 2, x_refs[2], 0))
    for tile, layer, at, x_ref, x_base in shares:
        valid, first_inner = inner_of(n_col, nb_rows, nb_cols, tile, layer)
        n_slots = jnp.where(valid, places[at, SLOTS], 0)
        list_pairs(todo, 0, places, at, n_slots, first_inner, slots_of, n_of, nb_rows, nb_cols)
        multiply_pairs(todo, 0, x_ref, y_blocks, acc, sums, x_base)


def list_scratch(n_row, nb_rows, nb_cols, shares):
    return [
        pltpu.SMEM((n_row * nb_rows * 8,), jnp.int32),
        pltpu.SMEM((n_row * nb_rows,), jnp.int32),
        pltpu.VMEM((shares, BLK), jnp.int32),
        pltpu.SMEM((shares, BLK), jnp.int32),
        pltpu.SMEM((1, SLOTS * nb_cols + 1 + UNROLL), jnp.int32),
    ]


def multiply_first(place, near, ys, xs, n_row, n_col, nb_rows, nb_cols):
    shares = len(near) + len(xs)
    return pl.pallas_call(
        functools.partial(first_kernel, near, n_col, nb_rows, nb_cols),
        out_shape=[
            jax.ShapeDtypeStruct((nb_rows * nb_cols + 1, BLK, BLK), jnp.float32),
            jax.ShapeDtypeStruct((nb_cols + 1, 8, BLK), jnp.float32),
            jax.ShapeDtypeStruct((n_row * ROWS, BLK), jnp.bfloat16),
        ],
        in_specs=[SMEM] + [ANY] * len(near) + [VMEM] * len(xs),
        out_specs=[VMEM] * 3,
        scratch_shapes=list_scratch(n_row, nb_rows, nb_cols, shares)
        + [pltpu.SemaphoreType.DMA((len(near),)), pltpu.SemaphoreType.DMA],
        compiler_params=pltpu.CompilerParams(vmem_limit_bytes=24 * MIB),
        cost_estimate=SMALL,
        name="multiply_first",
    )(place, *[ys[m] for m in near], *xs)


def second_kernel(near, n_row, n_col, nb_rows, nb_cols, x_kinds, place_ref, *refs):
    distant = [m for m in range(n_row) if m not in near]
    y_refs, refs = refs[: len(distant)], refs[len(distant) :]
    x_refs, refs = refs[: len(x_kinds)], refs[len(x_kinds) :]
    acc, sums, y_blocks, slots_of, n_of, heads, places, todo, y_sems, smem_sem = refs[3:]
    r, c, l = place_ref[0], place_ref[1], place_ref[2]
    copies = []
    for at, (m, y_ref) in enumerate(zip(distant, y_refs)):
        copies.append(pltpu.make_async_copy(y_ref, tile_rows(y_blocks, jnp.bitwise_xor(r, m)), y_sems.at[at]))
        copies[-1].start()
    for copy in copies:
        copy.wait()
    headers = column_headers(y_blocks, r, n_row) + [ref[0:HEAD, :] for ref in x_refs]
    read_headers(headers, heads, places, smem_sem).wait()
    list_column(slots_of, n_of, places, [(m, m) for m in range(n_row)], r, nb_rows)
    shares = [((0, False, False, True), 0, y_blocks, r * ROWS)]
    shares += [(kind, n_row + at, x_ref, 0) for at, (kind, x_ref) in enumerate(zip(x_kinds, x_refs))]
    for (step, odd, other, rest), at, x_ref, x_base in shares:
        tile = chain_tile(c, step, odd)
        valid, first_inner = inner_of(n_col, nb_rows, nb_cols, tile, 1 - l if other else l)
        if rest:
            for m in near:
                valid = jnp.logical_and(valid, jnp.bitwise_xor(tile, r) != m)
        n_slots = jnp.where(valid, places[at, SLOTS], 0)
        list_pairs(todo, 0, places, at, n_slots, first_inner, slots_of, n_of, nb_rows, nb_cols)
        multiply_pairs(todo, 0, x_ref, y_blocks, acc, sums, x_base)


def multiply_second(place, near, ys, xs, x_kinds, acc, sums, y_blocks, n_col, nb_rows, nb_cols):
    n_row = len(ys)
    distant = [ys[m] for m in range(n_row) if m not in near]
    operands = [place, *distant, *xs, acc, sums, y_blocks]
    lists = list_scratch(n_row, nb_rows, nb_cols, n_row + len(xs))
    return pl.pallas_call(
        functools.partial(second_kernel, near, n_row, n_col, nb_rows, nb_cols, x_kinds),
        out_shape=[jax.ShapeDtypeStruct(x.shape, x.dtype) for x in (acc, sums, y_blocks)]
        + [jax.ShapeDtypeStruct(x.shape, x.dtype) for x in lists[:2]],
        in_specs=[SMEM] + [ANY] * len(distant) + [VMEM] * (len(xs) + 3),
        out_specs=[VMEM] * 3 + [SMEM] * 2,
        input_output_aliases={len(operands) - 3 + at: at for at in range(3)},
        scratch_shapes=lists[2:] + [pltpu.SemaphoreType.DMA((len(distant),)), pltpu.SemaphoreType.DMA],
        compiler_params=pltpu.CompilerParams(vmem_limit_bytes=24 * MIB),
        cost_estimate=SMALL,
        name="multiply_second",
    )(*operands)


def late_kernel(n_col, nb_rows, nb_cols, x_kinds, is_last, place_ref, slots_of, n_of, y_blocks, *refs):
    x_refs, refs = refs[: len(x_kinds)], refs[len(x_kinds) :]
    _, before_sums, acc = refs[:3]
    sums, heads, places, todo, smem_sem = refs[-5:]
    c, l = place_ref[1], place_ref[2]
    to_smem = read_headers([ref[0:HEAD, :] for ref in x_refs], heads, places, smem_sem)
    for j in range(sums.shape[0]):
        sums[j] = before_sums[j]
    to_smem.wait()
    for at, (x_ref, (step, odd, other)) in enumerate(zip(x_refs, x_kinds)):
        valid, first_inner = inner_of(n_col, nb_rows, nb_cols, chain_tile(c, step, odd), 1 - l if other else l)
        n_slots = jnp.where(valid, places[at, SLOTS], 0)
        list_pairs(todo, 0, places, at, n_slots, first_inner, slots_of, n_of, nb_rows, nb_cols)
        multiply_pairs(todo, 0, x_ref, y_blocks, acc, sums)
    if is_last:
        totals = refs[3]
        for j in range(nb_cols):
            totals[:, j * BLK : (j + 1) * BLK] = jnp.sum(sums[j], axis=0, keepdims=True)


def multiply_late(place, slots_of, n_of, y_blocks, xs, x_kinds, acc, sums, is_last, n_col, nb_rows, nb_cols):
    totals = jax.ShapeDtypeStruct((1, nb_cols * BLK), jnp.float32)
    same_sums = jax.ShapeDtypeStruct(sums.shape, sums.dtype)
    operands = [place, slots_of, n_of, y_blocks, *xs, acc, sums]
    return pl.pallas_call(
        functools.partial(late_kernel, n_col, nb_rows, nb_cols, x_kinds, is_last),
        out_shape=[jax.ShapeDtypeStruct(acc.shape, acc.dtype), totals if is_last else same_sums],
        in_specs=[SMEM] * 3 + [VMEM] * (len(operands) - 3),
        out_specs=[VMEM, VMEM],
        input_output_aliases={len(operands) - 2: 0},
        scratch_shapes=([pltpu.VMEM(sums.shape, jnp.float32)] if is_last else [])
        + list_scratch(0, nb_rows, nb_cols, len(xs))[2:]
        + [pltpu.SemaphoreType.DMA],
        compiler_params=pltpu.CompilerParams(vmem_limit_bytes=24 * MIB),
        cost_estimate=SMALL,
        name="multiply_last" if is_last else "multiply_late",
    )(*operands)


def scale_kernel(scaling, nb_rows, nb_cols, *refs):
    product, sums = refs[0], refs[1:-3]
    out, scaled, sems = refs[-3:]
    total = sums[0][...]
    for other in sums[1:]:
        total = total + other[...]
    factor = scaling / total

    def out_copy(i):
        rows = pl.ds(pl.multiple_of(i * BLK, BLK), BLK)
        return pltpu.make_async_copy(scaled.at[rows, :], out.at[rows, :], sems.at[i])

    def square(i, carry):
        for j in range(nb_cols):
            value = product[i * nb_cols + j]
            scaled[pl.ds(pl.multiple_of(i * BLK, BLK), BLK), j * BLK : (j + 1) * BLK] = (
                value * value * factor[:, j * BLK : (j + 1) * BLK]
            )
        out_copy(i).start()
        return carry

    lax.fori_loop(0, nb_rows, square, 0)

    def wait(i, carry):
        out_copy(i).wait()
        return carry

    lax.fori_loop(0, nb_rows, wait, 0)


def scale(product, sums, scaling, nb_rows, nb_cols):
    shape = (nb_rows * BLK, nb_cols * BLK)
    return pl.pallas_call(
        functools.partial(scale_kernel, scaling, nb_rows, nb_cols),
        out_shape=jax.ShapeDtypeStruct(shape, jnp.float32),
        in_specs=[VMEM] * (1 + len(sums)),
        out_specs=ANY,
        scratch_shapes=[pltpu.VMEM(shape, jnp.float32), pltpu.SemaphoreType.DMA((nb_rows,))],
        compiler_params=pltpu.CompilerParams(vmem_limit_bytes=16 * MIB),
        cost_estimate=pl.CostEstimate(flops=10**7, bytes_accessed=10 * 10**6, transcendentals=0),
        name="scale",
    )(product, *sums)


def even_tile(i, step):
    return i + step if i % 2 == 0 else i - step


def odd_tile(i, step):
    return i - step if i % 2 == 0 else i + step


def body(n_row, n_col, similarity, block_mask):
    nb_rows, nb_cols = block_mask.shape
    r, c, l = lax.axis_index("row"), lax.axis_index("col"), lax.axis_index("layer")
    place = jnp.stack([r, c, l]).astype(jnp.int32)
    mask = block_mask.T

    def holders(tile, step):
        return [i for i in range(n_col) if 0 <= tile(i, step) < n_col]

    def hop(x, tile, step):
        return lax.ppermute(x, "col", [(tile(i, 1), i) for i in holders(tile, step)])

    def sibling(x, cols):
        pairs = [(2 * i + layer, 2 * i + 1 - layer) for i in cols for layer in range(2)]
        return lax.ppermute(x, ("col", "layer"), pairs)

    own = compact(mask, similarity)
    even = hop(own, even_tile, 1)
    odd = hop(own, odd_tile, 1)
    near = [m for m in range(n_row) if m.bit_count() <= 1]
    ys = [own] + [None] * (n_row - 1)
    for m in near[1:]:
        ys[m] = lax.ppermute(own, "row", [(s, s ^ m) for s in range(n_row)])
    for m in range(1, n_row):
        if ys[m] is None:
            bit = 1 << (m.bit_length() - 1)
            ys[m] = lax.ppermute(ys[m ^ bit], "row", [(s, s ^ bit) for s in range(n_row)])
    first_xs = [sibling(own, range(n_col)), odd, even]
    shares = list(zip([(0, False, True, True), (1, True, False, True), (1, False, False, True)], first_xs))
    acc, sums, y_blocks = multiply_first(place, near, ys, first_xs, n_row, n_col, nb_rows, nb_cols)
    for step in range(1, n_col - 2):
        shares.append(((step, True, True, False), sibling(odd, holders(odd_tile, step))))
        shares.append(((step, False, True, False), sibling(even, holders(even_tile, step))))
        odd, even = hop(even, odd_tile, step + 1), hop(odd, even_tile, step + 1)
        shares += [((step + 1, True, False, False), odd), ((step + 1, False, False, False), even)]
    odd, even, sums = lax.optimization_barrier((odd, even, sums))
    last = hop(odd, even_tile, n_col - 1)
    x_kinds, xs = zip(*shares)
    acc, sums, y_blocks, slots_of, n_of = multiply_second(
        place, near, ys, xs, x_kinds, acc, sums, y_blocks, n_col, nb_rows, nb_cols
    )
    last, sums = lax.optimization_barrier((last, sums))
    other = sibling(last, holders(even_tile, n_col - 1))
    kinds = [(n_col - 1, False, False), (n_col - 2, True, True), (n_col - 2, False, True)]
    xs = [last, sibling(odd, holders(odd_tile, n_col - 2)), sibling(even, holders(even_tile, n_col - 2))]
    sizes = n_col, nb_rows, nb_cols
    acc, sums = multiply_late(place, slots_of, n_of, y_blocks, xs, kinds, acc, sums, False, *sizes)
    kinds = [(n_col - 1, False, True)]
    product, sums = multiply_late(place, slots_of, n_of, y_blocks, [other], kinds, acc, sums, True, *sizes)
    all_sums = [sums]
    for m in range(1, n_row):
        all_sums.append(lax.ppermute(sums, "row", [(s, s ^ m) for s in range(n_row)]))
    return scale(product, all_sums, float(nb_rows * BLK * n_row), nb_rows, nb_cols)


def solution(mesh):
    n_row, n_col = mesh.shape["row"], mesh.shape["col"]
    return jax.shard_map(
        functools.partial(body, n_row, n_col),
        mesh=mesh,
        in_specs=(P("row", ("col", "layer")), P("row", ("col", "layer"))),
        out_specs=P("row", ("col", "layer")),
        check_vma=False,
    )
```

```python
import functools

import jax
import jax.numpy as jnp
from jax import lax
from jax.experimental import pallas as pl
from jax.experimental.pallas import tpu as pltpu
from jax.sharding import PartitionSpec as P

BLK = 128
SLOTS = 18
SHARE = SLOTS * BLK
HEAD = 16
HALF = 9
ROWS = HEAD + SHARE
FIRST_ROWS = HEAD + HALF * BLK
UNROLL = 8
LAG = 3
MIB = 1024 * 1024

SMEM = pl.BlockSpec(memory_space=pltpu.SMEM)
VMEM = pl.BlockSpec(memory_space=pltpu.VMEM)
ANY = pl.BlockSpec(memory_space=pl.ANY)
SMALL = pl.CostEstimate(flops=10**8, bytes_accessed=10**6, transcendentals=0)


def compact_kernel(mask_ref, sim_ref, out_ref, slots, places, in_sems, out_sems):
    nb_cols, nb_rows = mask_ref.shape

    def slot_rows(ref, slot):
        return ref.at[pl.ds(pl.multiple_of(HEAD + slot * BLK, HEAD), BLK), :]

    def copy_in(slot, i, k):
        block = sim_ref.at[pl.ds(pl.multiple_of(i * BLK, BLK), BLK), pl.ds(k * BLK, BLK)]
        return pltpu.make_async_copy(block, slot_rows(slots, slot), in_sems.at[slot])

    def copy_out(slot):
        return pltpu.make_async_copy(slot_rows(slots, slot), slot_rows(out_ref, slot), out_sems.at[slot])

    def scan(i, count):
        for k in range(nb_cols):
            here = mask_ref[k, i]

            @pl.when(here != 0)
            def _():
                copy_in(count, i, k).start()
                places[count] = i * 8 + k

            count = count + here
        return count

    for slot in range(SLOTS):
        places[slot] = 0
    count = lax.fori_loop(0, nb_rows, scan, jnp.int32(0))
    lane = lax.broadcasted_iota(jnp.int32, (HEAD, BLK), 1)
    header = jnp.where(lane == SLOTS, count, 0)
    for slot in range(SLOTS):
        header = jnp.where(lane == slot, places[slot], header)
    slots[0:HEAD, :] = header.astype(jnp.float32).astype(slots.dtype)
    header_out = pltpu.make_async_copy(slots.at[pl.ds(0, HEAD), :], out_ref.at[pl.ds(0, HEAD), :], out_sems.at[SLOTS])
    header_out.start()

    def pass_on(slot, carry):
        copy_in(slot, 0, 0).wait()
        copy_out(slot).start()
        return carry

    def finish(slot, carry):
        copy_out(slot).wait()
        return carry

    lax.fori_loop(0, count, pass_on, 0)
    lax.fori_loop(0, count, finish, 0)
    header_out.wait()


def compact(mask, similarity):
    return pl.pallas_call(
        compact_kernel,
        out_shape=jax.ShapeDtypeStruct((ROWS, BLK), similarity.dtype),
        in_specs=[SMEM, ANY],
        out_specs=ANY,
        scratch_shapes=[
            pltpu.VMEM((ROWS, BLK), similarity.dtype),
            pltpu.SMEM((SLOTS,), jnp.int32),
            pltpu.SemaphoreType.DMA((SLOTS,)),
            pltpu.SemaphoreType.DMA((SLOTS + 1,)),
        ],
        cost_estimate=pl.CostEstimate(flops=0, bytes_accessed=2 * SHARE * BLK * 2, transcendentals=0),
        name="compact",
    )(mask, similarity)


def multiply_pairs(todo, share, x_ref, y_blocks, acc, sums, x_base=0):
    def multiply(step, carry):
        terms = []

        def add_term(packed, term):
            at = jnp.bitwise_and(packed, 127)
            j = jnp.bitwise_and(lax.shift_right_logical(packed, 19), 7)
            old = acc[at]
            new = old + term
            acc[at] = new
            sums[j] += jnp.sum((term * (old + new)).reshape(BLK // 8, 8, BLK), axis=0)

        for u in range(UNROLL):
            packed = todo[share, 1 + step * UNROLL + u]
            x = x_base + HEAD + lax.shift_right_logical(packed, 22) * BLK
            y = jnp.bitwise_and(lax.shift_right_logical(packed, 7), 4095) * HEAD
            x_block = x_ref[pl.ds(pl.multiple_of(x, HEAD), BLK), :]
            y_block = y_blocks[pl.ds(pl.multiple_of(y, HEAD), BLK), :]
            terms.append((packed, jnp.dot(x_block, y_block, preferred_element_type=jnp.float32)))
            if u >= LAG:
                add_term(*terms[u - LAG])
        for packed, term in terms[UNROLL - LAG :]:
            add_term(packed, term)
        return carry

    n_steps = lax.shift_right_logical(todo[share, 0] + UNROLL - 1, UNROLL.bit_length() - 1)
    lax.fori_loop(0, n_steps, multiply, 0)


def list_pairs(todo, share, places, at, n_slots, first_inner, slots_of, n_of, nb_rows, nb_cols, first_slot=0):
    def slot_pairs(slot, count):
        place = places[at, slot]
        k = first_inner + jnp.bitwise_and(place, 7)
        packed = (slot << 22) + lax.shift_right_logical(place, 3) * nb_cols

        n_pairs = n_of[k]

        def pair(n, carry):
            todo[share, 1 + count + n] = packed + slots_of[k * 8 + n]
            return carry

        pair(0, 0)
        pair(1, 0)
        lax.fori_loop(2, n_pairs, pair, 0)
        return count + n_pairs

    count = lax.fori_loop(first_slot, n_slots, slot_pairs, jnp.int32(0))
    for u in range(UNROLL):
        todo[share, 1 + count + u] = (first_slot << 22) + (nb_cols << 19) + nb_rows * nb_cols
    todo[share, 0] = count


def clear_blocks(ref):
    def clear(at, carry):
        ref[at] = jnp.zeros(ref.shape[1:], ref.dtype)
        return carry

    lax.fori_loop(0, ref.shape[0], clear, 0)


def read_headers(headers, heads, places):
    for at, header in enumerate(headers):
        heads[at : at + 1, :] = header.astype(jnp.float32)[0:1, :].astype(jnp.int32)
    for at in range(len(headers)):
        for slot in range(SLOTS + 1):
            places[at, slot] = heads[at, slot]


def inner_of(n_col, nb_rows, nb_cols, tile, layer):
    valid = jnp.logical_and(tile >= 0, tile < n_col)
    return valid, jnp.where(valid, tile, 0) * nb_rows + layer * nb_cols


def tile_rows(y_blocks, tile, rows=ROWS):
    return y_blocks.at[pl.ds(pl.multiple_of(tile * ROWS, HEAD), rows), :]


def column_headers(y_blocks, r, n_row):
    return [tile_rows(y_blocks, jnp.bitwise_xor(r, m), HEAD)[...] for m in range(n_row)]


def list_column(slots_of, n_of, places, sources, r, nb_rows):
    def no_slots(k, carry):
        n_of[k] = 0
        return carry

    lax.fori_loop(0, n_of.shape[0], no_slots, 0)
    for at, m in sources:
        tile = jnp.bitwise_xor(r, m)
        first = tile * (ROWS // HEAD) + 1

        def put(slot, carry):
            place = places[at, slot]
            k = tile * nb_rows + lax.shift_right_logical(place, 3)
            n = n_of[k]
            j = jnp.bitwise_and(place, 7)
            slots_of[k * 8 + n] = (j << 19) + ((first + slot * (BLK // HEAD)) << 7) + j
            n_of[k] = n + 1
            return carry

        lax.fori_loop(0, places[at, SLOTS], put, 0)


def chain_tile(c, step, odd):
    forward = 1 - 2 * jnp.bitwise_and(c, 1)
    return c - step * forward if odd else c + step * forward


def first_kernel(near, n_col, nb_rows, nb_cols, place_ref, *refs):
    own_ref, refs = refs[0], refs[1:]
    y_refs, refs = refs[: len(near) - 1], refs[len(near) - 1 :]
    x_refs, refs = refs[:2], refs[2:]
    acc, sums, y_blocks, slots_of, n_of, own_head, heads, places, todo, y_sems = refs
    r, c, l = place_ref[0], place_ref[1], place_ref[2]
    head_copy = pltpu.make_async_copy(own_ref.at[pl.ds(0, HEAD), :], own_head, y_sems.at[len(near)])
    head_copy.start()
    copies = []
    for at, (m, y_ref) in enumerate(zip(near, (own_ref, *y_refs))):
        copies.append(pltpu.make_async_copy(y_ref, tile_rows(y_blocks, jnp.bitwise_xor(r, m)), y_sems.at[at]))
        copies[-1].start()
    head_copy.wait()
    headers = [own_head[...]] + [ref[0:HEAD, :] for ref in (*y_refs, *x_refs)]
    read_headers(headers, heads, places)
    clear_blocks(acc)
    clear_blocks(sums)
    list_column(slots_of, n_of, places, list(enumerate(near)), r, nb_rows)
    for copy in copies:
        copy.wait()
    shares = [(c, l, 0, y_blocks, r * ROWS), (c, 1 - l, len(near), x_refs[0], 0)]
    shares.append((chain_tile(c, 1, False), l, len(near) + 1, x_refs[1], 0))
    for tile, layer, at, x_ref, x_base in shares:
        valid, first_inner = inner_of(n_col, nb_rows, nb_cols, tile, layer)
        n_slots = jnp.where(valid, places[at, SLOTS], 0)
        list_pairs(todo, 0, places, at, n_slots, first_inner, slots_of, n_of, nb_rows, nb_cols)
        multiply_pairs(todo, 0, x_ref, y_blocks, acc, sums, x_base)


def list_scratch(n_row, nb_rows, nb_cols, shares):
    return [
        pltpu.SMEM((n_row * nb_rows * 8,), jnp.int32),
        pltpu.SMEM((n_row * nb_rows,), jnp.int32),
        pltpu.VMEM((shares, BLK), jnp.int32),
        pltpu.SMEM((shares, BLK), jnp.int32),
        pltpu.SMEM((1, SLOTS * nb_cols + 1 + UNROLL), jnp.int32),
    ]


def multiply_first(place, near, ys, xs, n_row, n_col, nb_rows, nb_cols):
    shares = len(near) + len(xs)
    lists = list_scratch(n_row, nb_rows, nb_cols, shares)
    return pl.pallas_call(
        functools.partial(first_kernel, near, n_col, nb_rows, nb_cols),
        out_shape=[
            jax.ShapeDtypeStruct((nb_rows * nb_cols + 1, BLK, BLK), jnp.float32),
            jax.ShapeDtypeStruct((nb_cols + 1, 8, BLK), jnp.float32),
            jax.ShapeDtypeStruct((n_row * ROWS, BLK), jnp.bfloat16),
        ],
        in_specs=[SMEM, ANY] + [VMEM] * (shares - 1),
        out_specs=[VMEM] * 3,
        scratch_shapes=lists[:2]
        + [pltpu.VMEM((HEAD, BLK), jnp.bfloat16)]
        + lists[2:]
        + [pltpu.SemaphoreType.DMA((len(near) + 1,))],
        compiler_params=pltpu.CompilerParams(vmem_limit_bytes=24 * MIB),
        cost_estimate=SMALL,
        name="multiply_first",
    )(place, *[ys[m] for m in near], *xs)


def second_kernel(near, n_row, n_col, nb_rows, nb_cols, x_kinds, place_ref, *refs):
    distant = [m for m in range(n_row) if m not in near]
    y_refs, refs = refs[: len(distant)], refs[len(distant) :]
    x_refs, refs = refs[: len(x_kinds)], refs[len(x_kinds) :]
    half_refs, refs = refs[:2], refs[2:]
    acc, sums, y_blocks, slots_of, n_of, heads, places, todo, y_sems = refs[3:]
    r, c, l = place_ref[0], place_ref[1], place_ref[2]
    copies = []
    for at, (m, y_ref) in enumerate(zip(distant, y_refs)):
        copies.append(pltpu.make_async_copy(y_ref, tile_rows(y_blocks, jnp.bitwise_xor(r, m)), y_sems.at[at]))
        copies[-1].start()
    for copy in copies:
        copy.wait()
    headers = column_headers(y_blocks, r, n_row) + [ref[0:HEAD, :] for ref in (*x_refs, half_refs[0])]
    read_headers(headers, heads, places)
    list_column(slots_of, n_of, places, [(m, m) for m in range(n_row)], r, nb_rows)
    shares = [((0, False, False, True), 0, y_blocks, r * ROWS)]
    shares += [(kind, n_row + at, x_ref, 0) for at, (kind, x_ref) in enumerate(zip(x_kinds, x_refs))]
    for (step, odd, other, rest), at, x_ref, x_base in shares:
        tile = chain_tile(c, step, odd)
        valid, first_inner = inner_of(n_col, nb_rows, nb_cols, tile, 1 - l if other else l)
        if rest:
            for m in near:
                valid = jnp.logical_and(valid, jnp.bitwise_xor(tile, r) != m)
        n_slots = jnp.where(valid, places[at, SLOTS], 0)
        list_pairs(todo, 0, places, at, n_slots, first_inner, slots_of, n_of, nb_rows, nb_cols)
        multiply_pairs(todo, 0, x_ref, y_blocks, acc, sums, x_base)
    is_end = jnp.logical_or(c == 0, c == n_col - 1)
    step, at = n_col - 2, n_row + len(x_refs)
    tile = jnp.where(is_end, chain_tile(c, step, False), chain_tile(c, step, True))
    valid, first_inner = inner_of(n_col, nb_rows, nb_cols, tile, 1 - l)
    n_slots = jnp.where(valid, places[at, SLOTS], 0)
    for first_slot, end, x_ref, x_base in (
        (0, jnp.minimum(n_slots, HALF), half_refs[0], 0),
        (HALF, n_slots, half_refs[1], -FIRST_ROWS),
    ):
        list_pairs(todo, 0, places, at, end, first_inner, slots_of, n_of, nb_rows, nb_cols, first_slot)
        multiply_pairs(todo, 0, x_ref, y_blocks, acc, sums, x_base)


def multiply_second(place, near, ys, xs, x_kinds, halves, acc, sums, y_blocks, n_col, nb_rows, nb_cols):
    n_row = len(ys)
    distant = [ys[m] for m in range(n_row) if m not in near]
    operands = [place, *distant, *xs, *halves, acc, sums, y_blocks]
    lists = list_scratch(n_row, nb_rows, nb_cols, n_row + len(xs) + 1)
    return pl.pallas_call(
        functools.partial(second_kernel, near, n_row, n_col, nb_rows, nb_cols, x_kinds),
        out_shape=[jax.ShapeDtypeStruct(x.shape, x.dtype) for x in (acc, sums, y_blocks)]
        + [jax.ShapeDtypeStruct(x.shape, x.dtype) for x in lists[:2]],
        in_specs=[SMEM] + [ANY] * len(distant) + [VMEM] * (len(xs) + 5),
        out_specs=[VMEM] * 3 + [SMEM] * 2,
        input_output_aliases={len(operands) - 3 + at: at for at in range(3)},
        scratch_shapes=lists[2:] + [pltpu.SemaphoreType.DMA((len(distant),))],
        compiler_params=pltpu.CompilerParams(vmem_limit_bytes=24 * MIB),
        cost_estimate=SMALL,
        name="multiply_second",
    )(*operands)


def late_kernel(n_col, nb_rows, nb_cols, x_kinds, is_last, place_ref, slots_of, n_of, y_blocks, *refs):
    x_refs, refs = refs[: len(x_kinds)], refs[len(x_kinds) :]
    _, before_sums, acc = refs[:3]
    sums, heads, places, todo = refs[-4:]
    c, l = place_ref[1], place_ref[2]
    read_headers([ref[0:HEAD, :] for ref in x_refs], heads, places)
    for j in range(sums.shape[0]):
        sums[j] = before_sums[j]
    for at, (x_ref, (step, odd, other)) in enumerate(zip(x_refs, x_kinds)):
        valid, first_inner = inner_of(n_col, nb_rows, nb_cols, chain_tile(c, step, odd), 1 - l if other else l)
        n_slots = jnp.where(valid, places[at, SLOTS], 0)
        list_pairs(todo, 0, places, at, n_slots, first_inner, slots_of, n_of, nb_rows, nb_cols)
        multiply_pairs(todo, 0, x_ref, y_blocks, acc, sums)
    if is_last:
        totals = refs[3]
        for j in range(nb_cols):
            totals[:, j * BLK : (j + 1) * BLK] = jnp.sum(sums[j], axis=0, keepdims=True)


def multiply_late(place, slots_of, n_of, y_blocks, xs, x_kinds, acc, sums, is_last, n_col, nb_rows, nb_cols):
    totals = jax.ShapeDtypeStruct((1, nb_cols * BLK), jnp.float32)
    same_sums = jax.ShapeDtypeStruct(sums.shape, sums.dtype)
    operands = [place, slots_of, n_of, y_blocks, *xs, acc, sums]
    return pl.pallas_call(
        functools.partial(late_kernel, n_col, nb_rows, nb_cols, x_kinds, is_last),
        out_shape=[jax.ShapeDtypeStruct(acc.shape, acc.dtype), totals if is_last else same_sums],
        in_specs=[SMEM] * 3 + [VMEM] * (len(operands) - 3),
        out_specs=[VMEM, VMEM],
        input_output_aliases={len(operands) - 2: 0},
        scratch_shapes=([pltpu.VMEM(sums.shape, jnp.float32)] if is_last else [])
        + list_scratch(0, nb_rows, nb_cols, len(xs))[2:],
        compiler_params=pltpu.CompilerParams(vmem_limit_bytes=24 * MIB),
        cost_estimate=SMALL,
        name="multiply_last" if is_last else "multiply_late",
    )(*operands)


def scale_kernel(scaling, nb_rows, nb_cols, *refs):
    product, sums = refs[0], refs[1:-3]
    out, scaled, sems = refs[-3:]
    total = sums[0][...]
    for other in sums[1:]:
        total = total + other[...]
    factor = scaling / total

    def out_copy(i):
        rows = pl.ds(pl.multiple_of(i * BLK, BLK), BLK)
        return pltpu.make_async_copy(scaled.at[rows, :], out.at[rows, :], sems.at[i])

    def square(i, carry):
        for j in range(nb_cols):
            value = product[i * nb_cols + j]
            scaled[pl.ds(pl.multiple_of(i * BLK, BLK), BLK), j * BLK : (j + 1) * BLK] = (
                value * value * factor[:, j * BLK : (j + 1) * BLK]
            )
        out_copy(i).start()
        return carry

    lax.fori_loop(0, nb_rows, square, 0)

    def wait(i, carry):
        out_copy(i).wait()
        return carry

    lax.fori_loop(0, nb_rows, wait, 0)


def scale(product, sums, scaling, nb_rows, nb_cols):
    shape = (nb_rows * BLK, nb_cols * BLK)
    return pl.pallas_call(
        functools.partial(scale_kernel, scaling, nb_rows, nb_cols),
        out_shape=jax.ShapeDtypeStruct(shape, jnp.float32),
        in_specs=[VMEM] * (1 + len(sums)),
        out_specs=ANY,
        scratch_shapes=[pltpu.VMEM(shape, jnp.float32), pltpu.SemaphoreType.DMA((nb_rows,))],
        compiler_params=pltpu.CompilerParams(vmem_limit_bytes=16 * MIB),
        cost_estimate=pl.CostEstimate(flops=10**7, bytes_accessed=10 * 10**6, transcendentals=0),
        name="scale",
    )(product, *sums)


def even_tile(i, step):
    return i + step if i % 2 == 0 else i - step


def odd_tile(i, step):
    return i - step if i % 2 == 0 else i + step


def body(n_row, n_col, similarity, block_mask):
    nb_rows, nb_cols = block_mask.shape
    r, c, l = lax.axis_index("row"), lax.axis_index("col"), lax.axis_index("layer")
    place = jnp.stack([r, c, l]).astype(jnp.int32)
    mask = block_mask.T

    def holders(tile, step):
        return [i for i in range(n_col) if 0 <= tile(i, step) < n_col]

    def hop(x, tile, step):
        return lax.ppermute(x, "col", [(tile(i, 1), i) for i in holders(tile, step)])

    def sibling(x, cols):
        pairs = [(2 * i + layer, 2 * i + 1 - layer) for i in cols for layer in range(2)]
        return lax.ppermute(x, ("col", "layer"), pairs)

    own = compact(mask, similarity)
    even = hop(own, even_tile, 1)
    odd = hop(own, odd_tile, 1)
    near = [m for m in range(n_row) if m.bit_count() <= 1]
    ys = [own] + [None] * (n_row - 1)
    for m in near[1:]:
        ys[m] = lax.ppermute(own, "row", [(s, s ^ m) for s in range(n_row)])
    for m in range(1, n_row):
        if ys[m] is None:
            bit = 1 << (m.bit_length() - 1)
            ys[m] = lax.ppermute(ys[m ^ bit], "row", [(s, s ^ bit) for s in range(n_row)])
    first_xs = [sibling(own, range(n_col)), even]
    shares = [((0, False, True, True), first_xs[0]), ((1, True, False, False), odd), ((1, False, False, True), even)]
    first_xs[1], _ = lax.optimization_barrier((even, odd))
    acc, sums, y_blocks = multiply_first(place, near, ys, first_xs, n_row, n_col, nb_rows, nb_cols)
    for step in range(1, n_col - 2):
        shares.append(((step, True, True, False), sibling(odd, holders(odd_tile, step))))
        shares.append(((step, False, True, False), sibling(even, holders(even_tile, step))))
        odd, even = hop(even, odd_tile, step + 1), hop(odd, even_tile, step + 1)
        shares += [((step + 1, True, False, False), odd), ((step + 1, False, False, False), even)]
    odd, sums = lax.optimization_barrier((odd, sums))
    last = hop(odd, even_tile, n_col - 1)
    arrived = jnp.where(jnp.logical_or(c == 0, c == n_col - 1), even, odd)
    halves = [sibling(arrived[:FIRST_ROWS], range(n_col)), sibling(arrived[FIRST_ROWS:], range(n_col))]
    x_kinds, xs = zip(*shares)
    acc, sums, y_blocks, slots_of, n_of = multiply_second(
        place, near, ys, xs, x_kinds, halves, acc, sums, y_blocks, n_col, nb_rows, nb_cols
    )
    last, sums = lax.optimization_barrier((last, sums))
    other = sibling(last, holders(even_tile, n_col - 1))
    kinds = [(n_col - 1, False, False)]
    sizes = n_col, nb_rows, nb_cols
    acc, sums = multiply_late(place, slots_of, n_of, y_blocks, [last], kinds, acc, sums, False, *sizes)
    kinds = [(n_col - 1, False, True)]
    product, sums = multiply_late(place, slots_of, n_of, y_blocks, [other], kinds, acc, sums, True, *sizes)
    all_sums = [sums]
    for m in range(1, n_row):
        all_sums.append(lax.ppermute(sums, "row", [(s, s ^ m) for s in range(n_row)]))
    return scale(product, all_sums, float(nb_rows * BLK * n_row), nb_rows, nb_cols)


def solution(mesh):
    n_row, n_col = mesh.shape["row"], mesh.shape["col"]
    return jax.shard_map(
        functools.partial(body, n_row, n_col),
        mesh=mesh,
        in_specs=(P("row", ("col", "layer")), P("row", ("col", "layer"))),
        out_specs=P("row", ("col", "layer")),
        check_vma=False,
    )
```

```python
import functools

import jax
import jax.numpy as jnp
from jax import lax
from jax.experimental import pallas as pl
from jax.experimental.pallas import tpu as pltpu
from jax.sharding import PartitionSpec as P

BLK = 128
SLOTS = 18
SHARE = SLOTS * BLK
HEAD = 16
HALF = 9
ROWS = HEAD + SHARE
FIRST_ROWS = HEAD + HALF * BLK
UNROLL = 8
LAG = 3
MIB = 1024 * 1024

SMEM = pl.BlockSpec(memory_space=pltpu.SMEM)
VMEM = pl.BlockSpec(memory_space=pltpu.VMEM)
ANY = pl.BlockSpec(memory_space=pl.ANY)
SMALL = pl.CostEstimate(flops=10**8, bytes_accessed=10**6, transcendentals=0)


def compact_kernel(mask_ref, sim_ref, out_ref, places, sems):
    nb_cols, nb_rows = mask_ref.shape

    def block_copy(slot, i, k):
        block = sim_ref.at[pl.ds(pl.multiple_of(i * BLK, BLK), BLK), pl.ds(k * BLK, BLK)]
        return pltpu.make_async_copy(
            block, out_ref.at[pl.ds(pl.multiple_of(HEAD + slot * BLK, HEAD), BLK), :], sems.at[slot]
        )

    def scan(i, count):
        for k in range(nb_cols):
            here = mask_ref[k, i]

            @pl.when(here != 0)
            def _():
                block_copy(count, i, k).start()
                places[count] = i * 8 + k

            count = count + here
        return count

    for slot in range(SLOTS):
        places[slot] = 0
    count = lax.fori_loop(0, nb_rows, scan, jnp.int32(0))
    lane = lax.broadcasted_iota(jnp.int32, (HEAD, BLK), 1)
    header = jnp.where(lane == SLOTS, count, 0)
    for slot in range(SLOTS):
        header = jnp.where(lane == slot, places[slot], header)
    out_ref[0:HEAD, :] = header.astype(jnp.float32).astype(out_ref.dtype)

    def wait(slot, carry):
        block_copy(slot, 0, 0).wait()
        return carry

    lax.fori_loop(0, count, wait, 0)


def compact(mask, similarity):
    return pl.pallas_call(
        compact_kernel,
        out_shape=pltpu.VMEM((ROWS, BLK), similarity.dtype),
        in_specs=[SMEM, ANY],
        out_specs=VMEM,
        scratch_shapes=[pltpu.SMEM((SLOTS,), jnp.int32), pltpu.SemaphoreType.DMA((SLOTS,))],
        cost_estimate=pl.CostEstimate(flops=0, bytes_accessed=2 * SHARE * BLK * 2, transcendentals=0),
        name="compact",
    )(mask, similarity)


def multiply_pairs(todo, share, x_ref, y_blocks, acc, sums, x_base=0):
    def multiply(step, carry):
        terms = []

        def add_term(packed, term):
            at = jnp.bitwise_and(packed, 127)
            j = jnp.bitwise_and(lax.shift_right_logical(packed, 19), 7)
            old = acc[at]
            new = old + term
            acc[at] = new
            sums[j] += jnp.sum((term * (old + new)).reshape(BLK // 8, 8, BLK), axis=0)

        for u in range(UNROLL):
            packed = todo[share, 1 + step * UNROLL + u]
            x = x_base + HEAD + lax.shift_right_logical(packed, 22) * BLK
            y = jnp.bitwise_and(lax.shift_right_logical(packed, 7), 4095) * HEAD
            x_block = x_ref[pl.ds(pl.multiple_of(x, HEAD), BLK), :]
            y_block = y_blocks[pl.ds(pl.multiple_of(y, HEAD), BLK), :]
            terms.append((packed, jnp.dot(x_block, y_block, preferred_element_type=jnp.float32)))
            if u >= LAG:
                add_term(*terms[u - LAG])
        for packed, term in terms[UNROLL - LAG :]:
            add_term(packed, term)
        return carry

    n_steps = lax.shift_right_logical(todo[share, 0] + UNROLL - 1, UNROLL.bit_length() - 1)
    lax.fori_loop(0, n_steps, multiply, 0)


def list_pairs(todo, share, places, at, n_slots, first_inner, slots_of, n_of, nb_rows, nb_cols, first_slot=0):
    def slot_pairs(slot, count):
        place = places[at, slot]
        k = first_inner + jnp.bitwise_and(place, 7)
        packed = (slot << 22) + lax.shift_right_logical(place, 3) * nb_cols

        n_pairs = n_of[k]

        def pair(n, carry):
            todo[share, 1 + count + n] = packed + slots_of[k * 8 + n]
            return carry

        pair(0, 0)
        pair(1, 0)
        lax.fori_loop(2, n_pairs, pair, 0)
        return count + n_pairs

    count = lax.fori_loop(first_slot, n_slots, slot_pairs, jnp.int32(0))
    for u in range(UNROLL):
        todo[share, 1 + count + u] = (first_slot << 22) + (nb_cols << 19) + nb_rows * nb_cols
    todo[share, 0] = count


def clear_blocks(ref):
    def clear(at, carry):
        ref[at] = jnp.zeros(ref.shape[1:], ref.dtype)
        return carry

    lax.fori_loop(0, ref.shape[0], clear, 0)


def read_headers(headers, heads, places):
    for at, header in enumerate(headers):
        heads[at : at + 1, :] = header.astype(jnp.float32)[0:1, :].astype(jnp.int32)
    for at in range(len(headers)):
        for slot in range(SLOTS + 1):
            places[at, slot] = heads[at, slot]


def inner_of(n_col, nb_rows, nb_cols, tile, layer):
    valid = jnp.logical_and(tile >= 0, tile < n_col)
    return valid, jnp.where(valid, tile, 0) * nb_rows + layer * nb_cols


def tile_rows(y_blocks, tile, rows=ROWS):
    return y_blocks.at[pl.ds(pl.multiple_of(tile * ROWS, HEAD), rows), :]


def column_headers(y_blocks, r, n_row):
    return [tile_rows(y_blocks, jnp.bitwise_xor(r, m), HEAD)[...] for m in range(n_row)]


def list_column(slots_of, n_of, places, sources, r, nb_rows):
    def no_slots(k, carry):
        n_of[k] = 0
        return carry

    lax.fori_loop(0, n_of.shape[0], no_slots, 0)
    for at, m in sources:
        tile = jnp.bitwise_xor(r, m)
        first = tile * (ROWS // HEAD) + 1

        def put(slot, carry):
            place = places[at, slot]
            k = tile * nb_rows + lax.shift_right_logical(place, 3)
            n = n_of[k]
            j = jnp.bitwise_and(place, 7)
            slots_of[k * 8 + n] = (j << 19) + ((first + slot * (BLK // HEAD)) << 7) + j
            n_of[k] = n + 1
            return carry

        lax.fori_loop(0, places[at, SLOTS], put, 0)


def chain_tile(c, step, odd):
    forward = 1 - 2 * jnp.bitwise_and(c, 1)
    return c - step * forward if odd else c + step * forward


def first_kernel(near, n_col, nb_rows, nb_cols, place_ref, *refs):
    own_ref, refs = refs[0], refs[1:]
    y_refs, refs = refs[: len(near) - 1], refs[len(near) - 1 :]
    x_refs, refs = refs[:2], refs[2:]
    acc, sums, y_blocks, slots_of, n_of, own_head, heads, places, todo, y_sems = refs
    r, c, l = place_ref[0], place_ref[1], place_ref[2]
    head_copy = pltpu.make_async_copy(own_ref.at[pl.ds(0, HEAD), :], own_head, y_sems.at[len(near)])
    head_copy.start()
    copies = []
    for at, (m, y_ref) in enumerate(zip(near, (own_ref, *y_refs))):
        copies.append(pltpu.make_async_copy(y_ref, tile_rows(y_blocks, jnp.bitwise_xor(r, m)), y_sems.at[at]))
        copies[-1].start()
    head_copy.wait()
    headers = [own_head[...]] + [ref[0:HEAD, :] for ref in (*y_refs, *x_refs)]
    read_headers(headers, heads, places)
    clear_blocks(acc)
    clear_blocks(sums)
    list_column(slots_of, n_of, places, list(enumerate(near)), r, nb_rows)
    for copy in copies:
        copy.wait()
    shares = [(c, l, 0, y_blocks, r * ROWS), (c, 1 - l, len(near), x_refs[0], 0)]
    shares.append((chain_tile(c, 1, False), l, len(near) + 1, x_refs[1], 0))
    for tile, layer, at, x_ref, x_base in shares:
        valid, first_inner = inner_of(n_col, nb_rows, nb_cols, tile, layer)
        n_slots = jnp.where(valid, places[at, SLOTS], 0)
        list_pairs(todo, 0, places, at, n_slots, first_inner, slots_of, n_of, nb_rows, nb_cols)
        multiply_pairs(todo, 0, x_ref, y_blocks, acc, sums, x_base)


def list_scratch(n_row, nb_rows, nb_cols, shares):
    return [
        pltpu.SMEM((n_row * nb_rows * 8,), jnp.int32),
        pltpu.SMEM((n_row * nb_rows,), jnp.int32),
        pltpu.VMEM((shares, BLK), jnp.int32),
        pltpu.SMEM((shares, BLK), jnp.int32),
        pltpu.SMEM((1, SLOTS * nb_cols + 1 + UNROLL), jnp.int32),
    ]


def multiply_first(place, near, ys, xs, n_row, n_col, nb_rows, nb_cols):
    shares = len(near) + len(xs)
    lists = list_scratch(n_row, nb_rows, nb_cols, shares)
    return pl.pallas_call(
        functools.partial(first_kernel, near, n_col, nb_rows, nb_cols),
        out_shape=[
            jax.ShapeDtypeStruct((nb_rows * nb_cols + 1, BLK, BLK), jnp.float32),
            jax.ShapeDtypeStruct((nb_cols + 1, 8, BLK), jnp.float32),
            jax.ShapeDtypeStruct((n_row * ROWS, BLK), jnp.bfloat16),
        ],
        in_specs=[SMEM, ANY] + [VMEM] * (shares - 1),
        out_specs=[VMEM] * 3,
        scratch_shapes=lists[:2]
        + [pltpu.VMEM((HEAD, BLK), jnp.bfloat16)]
        + lists[2:]
        + [pltpu.SemaphoreType.DMA((len(near) + 1,))],
        compiler_params=pltpu.CompilerParams(vmem_limit_bytes=24 * MIB),
        cost_estimate=SMALL,
        name="multiply_first",
    )(place, *[ys[m] for m in near], *xs)


def second_kernel(near, n_row, n_col, nb_rows, nb_cols, x_kinds, place_ref, *refs):
    distant = [m for m in range(n_row) if m not in near]
    y_refs, refs = refs[: len(distant)], refs[len(distant) :]
    x_refs, refs = refs[: len(x_kinds)], refs[len(x_kinds) :]
    half_refs, refs = refs[:2], refs[2:]
    acc, sums, y_blocks, slots_of, n_of, heads, places, todo, y_sems = refs[3:]
    r, c, l = place_ref[0], place_ref[1], place_ref[2]
    copies = []
    for at, (m, y_ref) in enumerate(zip(distant, y_refs)):
        copies.append(pltpu.make_async_copy(y_ref, tile_rows(y_blocks, jnp.bitwise_xor(r, m)), y_sems.at[at]))
        copies[-1].start()
    for copy in copies:
        copy.wait()
    headers = column_headers(y_blocks, r, n_row) + [ref[0:HEAD, :] for ref in (*x_refs, half_refs[0])]
    read_headers(headers, heads, places)
    list_column(slots_of, n_of, places, [(m, m) for m in range(n_row)], r, nb_rows)
    shares = [((0, False, False, True), 0, y_blocks, r * ROWS)]
    shares += [(kind, n_row + at, x_ref, 0) for at, (kind, x_ref) in enumerate(zip(x_kinds, x_refs))]
    for (step, odd, other, rest), at, x_ref, x_base in shares:
        tile = chain_tile(c, step, odd)
        valid, first_inner = inner_of(n_col, nb_rows, nb_cols, tile, 1 - l if other else l)
        if rest:
            for m in near:
                valid = jnp.logical_and(valid, jnp.bitwise_xor(tile, r) != m)
        n_slots = jnp.where(valid, places[at, SLOTS], 0)
        list_pairs(todo, 0, places, at, n_slots, first_inner, slots_of, n_of, nb_rows, nb_cols)
        multiply_pairs(todo, 0, x_ref, y_blocks, acc, sums, x_base)
    is_end = jnp.logical_or(c == 0, c == n_col - 1)
    step, at = n_col - 2, n_row + len(x_refs)
    tile = jnp.where(is_end, chain_tile(c, step, False), chain_tile(c, step, True))
    valid, first_inner = inner_of(n_col, nb_rows, nb_cols, tile, 1 - l)
    n_slots = jnp.where(valid, places[at, SLOTS], 0)
    for first_slot, end, x_ref, x_base in (
        (0, jnp.minimum(n_slots, HALF), half_refs[0], 0),
        (HALF, n_slots, half_refs[1], -FIRST_ROWS),
    ):
        list_pairs(todo, 0, places, at, end, first_inner, slots_of, n_of, nb_rows, nb_cols, first_slot)
        multiply_pairs(todo, 0, x_ref, y_blocks, acc, sums, x_base)


def multiply_second(place, near, ys, xs, x_kinds, halves, acc, sums, y_blocks, n_col, nb_rows, nb_cols):
    n_row = len(ys)
    distant = [ys[m] for m in range(n_row) if m not in near]
    operands = [place, *distant, *xs, *halves, acc, sums, y_blocks]
    lists = list_scratch(n_row, nb_rows, nb_cols, n_row + len(xs) + 1)
    return pl.pallas_call(
        functools.partial(second_kernel, near, n_row, n_col, nb_rows, nb_cols, x_kinds),
        out_shape=[jax.ShapeDtypeStruct(x.shape, x.dtype) for x in (acc, sums, y_blocks)]
        + [jax.ShapeDtypeStruct(x.shape, x.dtype) for x in lists[:2]],
        in_specs=[SMEM] + [ANY] * len(distant) + [VMEM] * (len(xs) + 5),
        out_specs=[VMEM] * 3 + [SMEM] * 2,
        input_output_aliases={len(operands) - 3 + at: at for at in range(3)},
        scratch_shapes=lists[2:] + [pltpu.SemaphoreType.DMA((len(distant),))],
        compiler_params=pltpu.CompilerParams(vmem_limit_bytes=24 * MIB),
        cost_estimate=SMALL,
        name="multiply_second",
    )(*operands)


def late_kernel(n_col, nb_rows, nb_cols, x_kinds, is_last, place_ref, slots_of, n_of, y_blocks, *refs):
    x_refs, refs = refs[: len(x_kinds)], refs[len(x_kinds) :]
    _, before_sums, acc = refs[:3]
    sums, heads, places, todo = refs[-4:]
    c, l = place_ref[1], place_ref[2]
    read_headers([ref[0:HEAD, :] for ref in x_refs], heads, places)
    for j in range(sums.shape[0]):
        sums[j] = before_sums[j]
    for at, (x_ref, (step, odd, other)) in enumerate(zip(x_refs, x_kinds)):
        valid, first_inner = inner_of(n_col, nb_rows, nb_cols, chain_tile(c, step, odd), 1 - l if other else l)
        n_slots = jnp.where(valid, places[at, SLOTS], 0)
        list_pairs(todo, 0, places, at, n_slots, first_inner, slots_of, n_of, nb_rows, nb_cols)
        multiply_pairs(todo, 0, x_ref, y_blocks, acc, sums)
    if is_last:
        totals = refs[3]
        for j in range(nb_cols):
            totals[:, j * BLK : (j + 1) * BLK] = jnp.sum(sums[j], axis=0, keepdims=True)


def multiply_late(place, slots_of, n_of, y_blocks, xs, x_kinds, acc, sums, is_last, n_col, nb_rows, nb_cols):
    totals = jax.ShapeDtypeStruct((1, nb_cols * BLK), jnp.float32)
    same_sums = jax.ShapeDtypeStruct(sums.shape, sums.dtype)
    operands = [place, slots_of, n_of, y_blocks, *xs, acc, sums]
    return pl.pallas_call(
        functools.partial(late_kernel, n_col, nb_rows, nb_cols, x_kinds, is_last),
        out_shape=[jax.ShapeDtypeStruct(acc.shape, acc.dtype), totals if is_last else same_sums],
        in_specs=[SMEM] * 3 + [VMEM] * (len(operands) - 3),
        out_specs=[VMEM, VMEM],
        input_output_aliases={len(operands) - 2: 0},
        scratch_shapes=([pltpu.VMEM(sums.shape, jnp.float32)] if is_last else [])
        + list_scratch(0, nb_rows, nb_cols, len(xs))[2:],
        compiler_params=pltpu.CompilerParams(vmem_limit_bytes=24 * MIB),
        cost_estimate=SMALL,
        name="multiply_last" if is_last else "multiply_late",
    )(*operands)


def scale_kernel(scaling, nb_rows, nb_cols, *refs):
    product, sums = refs[0], refs[1:-3]
    out, scaled, sems = refs[-3:]
    total = sums[0][...]
    for other in sums[1:]:
        total = total + other[...]
    factor = scaling / total

    def out_copy(i):
        rows = pl.ds(pl.multiple_of(i * BLK, BLK), BLK)
        return pltpu.make_async_copy(scaled.at[rows, :], out.at[rows, :], sems.at[i])

    def square(i, carry):
        for j in range(nb_cols):
            value = product[i * nb_cols + j]
            scaled[pl.ds(pl.multiple_of(i * BLK, BLK), BLK), j * BLK : (j + 1) * BLK] = (
                value * value * factor[:, j * BLK : (j + 1) * BLK]
            )
        out_copy(i).start()
        return carry

    lax.fori_loop(0, nb_rows, square, 0)

    def wait(i, carry):
        out_copy(i).wait()
        return carry

    lax.fori_loop(0, nb_rows, wait, 0)


def scale(product, sums, scaling, nb_rows, nb_cols):
    shape = (nb_rows * BLK, nb_cols * BLK)
    return pl.pallas_call(
        functools.partial(scale_kernel, scaling, nb_rows, nb_cols),
        out_shape=jax.ShapeDtypeStruct(shape, jnp.float32),
        in_specs=[VMEM] * (1 + len(sums)),
        out_specs=ANY,
        scratch_shapes=[pltpu.VMEM(shape, jnp.float32), pltpu.SemaphoreType.DMA((nb_rows,))],
        compiler_params=pltpu.CompilerParams(vmem_limit_bytes=16 * MIB),
        cost_estimate=pl.CostEstimate(flops=10**7, bytes_accessed=10 * 10**6, transcendentals=0),
        name="scale",
    )(product, *sums)


def even_tile(i, step):
    return i + step if i % 2 == 0 else i - step


def odd_tile(i, step):
    return i - step if i % 2 == 0 else i + step


def body(n_row, n_col, similarity, block_mask):
    nb_rows, nb_cols = block_mask.shape
    r, c, l = lax.axis_index("row"), lax.axis_index("col"), lax.axis_index("layer")
    place = jnp.stack([r, c, l]).astype(jnp.int32)
    mask = block_mask.T

    def hop(x, tile):
        targets = [tile(i, 1) if 0 <= tile(i, 1) < n_col else i for i in range(n_col)]
        return lax.ppermute(x, "col", list(enumerate(targets)))

    def sibling(x):
        return lax.ppermute(x, "layer", [(0, 1), (1, 0)])

    own = compact(mask, similarity)
    even = hop(own, even_tile)
    odd = hop(own, odd_tile)
    near = [m for m in range(n_row) if m.bit_count() <= 1]
    ys = [own] + [None] * (n_row - 1)
    for m in near[1:]:
        ys[m] = lax.ppermute(own, "row", [(s, s ^ m) for s in range(n_row)])
    for m in range(1, n_row):
        if ys[m] is None:
            bit = 1 << (m.bit_length() - 1)
            ys[m] = lax.ppermute(ys[m ^ bit], "row", [(s, s ^ bit) for s in range(n_row)])
    first_xs = [sibling(own), even]
    shares = [((0, False, True, True), first_xs[0]), ((1, True, False, False), odd), ((1, False, False, True), even)]
    first_xs[1], _ = lax.optimization_barrier((even, odd))
    acc, sums, y_blocks = multiply_first(place, near, ys, first_xs, n_row, n_col, nb_rows, nb_cols)
    for step in range(1, n_col - 2):
        shares.append(((step, True, True, False), sibling(odd)))
        shares.append(((step, False, True, False), sibling(even)))
        odd, even = hop(even, odd_tile), hop(odd, even_tile)
        shares += [((step + 1, True, False, False), odd), ((step + 1, False, False, False), even)]
    odd, sums = lax.optimization_barrier((odd, sums))
    last = hop(odd, even_tile)
    arrived = jnp.where(jnp.logical_or(c == 0, c == n_col - 1), even, odd)
    halves = [sibling(arrived[:FIRST_ROWS]), sibling(arrived[FIRST_ROWS:])]
    x_kinds, xs = zip(*shares)
    acc, sums, y_blocks, slots_of, n_of = multiply_second(
        place, near, ys, xs, x_kinds, halves, acc, sums, y_blocks, n_col, nb_rows, nb_cols
    )
    last, sums = lax.optimization_barrier((last, sums))
    other = sibling(last)
    kinds = [(n_col - 1, False, False)]
    sizes = n_col, nb_rows, nb_cols
    acc, sums = multiply_late(place, slots_of, n_of, y_blocks, [last], kinds, acc, sums, False, *sizes)
    kinds = [(n_col - 1, False, True)]
    product, sums = multiply_late(place, slots_of, n_of, y_blocks, [other], kinds, acc, sums, True, *sizes)
    all_sums = [sums]
    for m in range(1, n_row):
        all_sums.append(lax.ppermute(sums, "row", [(s, s ^ m) for s in range(n_row)]))
    return scale(product, all_sums, float(nb_rows * BLK * n_row), nb_rows, nb_cols)


def solution(mesh):
    n_row, n_col = mesh.shape["row"], mesh.shape["col"]
    return jax.shard_map(
        functools.partial(body, n_row, n_col),
        mesh=mesh,
        in_specs=(P("row", ("col", "layer")), P("row", ("col", "layer"))),
        out_specs=P("row", ("col", "layer")),
        check_vma=False,
    )
```

```python
import functools

import jax
import jax.numpy as jnp
from jax import lax
from jax.experimental import pallas as pl
from jax.experimental.pallas import tpu as pltpu
from jax.sharding import PartitionSpec as P

BLK = 128
SLOTS = 18
SHARE = SLOTS * BLK
HEAD = 16
HALF = 9
ROWS = HEAD + SHARE
FIRST_ROWS = HEAD + HALF * BLK
UNROLL = 8
LAG = 3
MIB = 1024 * 1024

SMEM = pl.BlockSpec(memory_space=pltpu.SMEM)
VMEM = pl.BlockSpec(memory_space=pltpu.VMEM)
ANY = pl.BlockSpec(memory_space=pl.ANY)
SMALL = pl.CostEstimate(flops=10**8, bytes_accessed=10**6, transcendentals=0)


def compact_kernel(mask_ref, sim_ref, out_ref, places, sems):
    nb_cols, nb_rows = mask_ref.shape

    def block_copy(slot, i, k):
        block = sim_ref.at[pl.ds(pl.multiple_of(i * BLK, BLK), BLK), pl.ds(k * BLK, BLK)]
        return pltpu.make_async_copy(
            block, out_ref.at[pl.ds(pl.multiple_of(HEAD + slot * BLK, HEAD), BLK), :], sems.at[slot]
        )

    def scan(i, count):
        for k in range(nb_cols):
            here = mask_ref[k, i]

            @pl.when(here != 0)
            def _():
                block_copy(count, i, k).start()
                places[count] = i * 8 + k

            count = count + here
        return count

    for slot in range(SLOTS):
        places[slot] = 0
    count = lax.fori_loop(0, nb_rows, scan, jnp.int32(0))
    lane = lax.broadcasted_iota(jnp.int32, (HEAD, BLK), 1)
    header = jnp.where(lane == SLOTS, count, 0)
    for slot in range(SLOTS):
        header = jnp.where(lane == slot, places[slot], header)
    out_ref[0:HEAD, :] = header.astype(jnp.float32).astype(out_ref.dtype)

    def wait(slot, carry):
        block_copy(slot, 0, 0).wait()
        return carry

    lax.fori_loop(0, count, wait, 0)


def compact(mask, similarity):
    return pl.pallas_call(
        compact_kernel,
        out_shape=pltpu.VMEM((ROWS, BLK), similarity.dtype),
        in_specs=[SMEM, ANY],
        out_specs=VMEM,
        scratch_shapes=[pltpu.SMEM((SLOTS,), jnp.int32), pltpu.SemaphoreType.DMA((SLOTS,))],
        cost_estimate=pl.CostEstimate(flops=0, bytes_accessed=2 * SHARE * BLK * 2, transcendentals=0),
        name="compact",
    )(mask, similarity)


def multiply_pairs(todo, share, x_ref, y_blocks, acc, sums, x_base=0):
    def multiply(step, carry):
        terms = []

        def add_term(packed, term):
            at = jnp.bitwise_and(packed, 127)
            j = jnp.bitwise_and(lax.shift_right_logical(packed, 19), 7)
            old = acc[at]
            new = old + term
            acc[at] = new
            sums[j] += jnp.sum((term * (old + new)).reshape(BLK // 8, 8, BLK), axis=0)

        for u in range(UNROLL):
            packed = todo[share, 1 + step * UNROLL + u]
            x = x_base + HEAD + lax.shift_right_logical(packed, 22) * BLK
            y = jnp.bitwise_and(lax.shift_right_logical(packed, 7), 4095) * HEAD
            x_block = x_ref[pl.ds(pl.multiple_of(x, HEAD), BLK), :]
            y_block = y_blocks[pl.ds(pl.multiple_of(y, HEAD), BLK), :]
            terms.append((packed, jnp.dot(x_block, y_block, preferred_element_type=jnp.float32)))
            if u >= LAG:
                add_term(*terms[u - LAG])
        for packed, term in terms[UNROLL - LAG :]:
            add_term(packed, term)
        return carry

    n_steps = lax.shift_right_logical(todo[share, 0] + UNROLL - 1, UNROLL.bit_length() - 1)
    lax.fori_loop(0, n_steps, multiply, 0)


def list_pairs(todo, share, places, at, n_slots, first_inner, slots_of, n_of, nb_rows, nb_cols, first_slot=0):
    def slot_pairs(slot, count):
        place = places[at, slot]
        k = first_inner + jnp.bitwise_and(place, 7)
        packed = (slot << 22) + lax.shift_right_logical(place, 3) * nb_cols

        n_pairs = n_of[k]

        def pair(n, carry):
            todo[share, 1 + count + n] = packed + slots_of[k * 8 + n]
            return carry

        pair(0, 0)
        pair(1, 0)
        lax.fori_loop(2, n_pairs, pair, 0)
        return count + n_pairs

    count = lax.fori_loop(first_slot, n_slots, slot_pairs, jnp.int32(0))
    for u in range(UNROLL):
        todo[share, 1 + count + u] = (first_slot << 22) + (nb_cols << 19) + nb_rows * nb_cols
    todo[share, 0] = count


def clear_blocks(ref):
    def clear(at, carry):
        ref[at] = jnp.zeros(ref.shape[1:], ref.dtype)
        return carry

    lax.fori_loop(0, ref.shape[0], clear, 0)


def read_headers(headers, heads, places):
    for at, header in enumerate(headers):
        heads[at : at + 1, :] = header.astype(jnp.float32)[0:1, :].astype(jnp.int32)
    for at in range(len(headers)):
        for slot in range(SLOTS + 1):
            places[at, slot] = heads[at, slot]


def inner_of(n_col, nb_rows, nb_cols, tile, layer):
    valid = jnp.logical_and(tile >= 0, tile < n_col)
    return valid, jnp.where(valid, tile, 0) * nb_rows + layer * nb_cols


def tile_rows(y_blocks, tile, rows=ROWS):
    return y_blocks.at[pl.ds(pl.multiple_of(tile * ROWS, HEAD), rows), :]


def column_headers(y_blocks, r, n_row):
    return [tile_rows(y_blocks, jnp.bitwise_xor(r, m), HEAD)[...] for m in range(n_row)]


def list_column(slots_of, n_of, places, sources, r, nb_rows):
    def no_slots(k, carry):
        n_of[k] = 0
        return carry

    lax.fori_loop(0, n_of.shape[0], no_slots, 0)
    for at, m in sources:
        tile = jnp.bitwise_xor(r, m)
        first = tile * (ROWS // HEAD) + 1

        def put(slot, carry):
            place = places[at, slot]
            k = tile * nb_rows + lax.shift_right_logical(place, 3)
            n = n_of[k]
            j = jnp.bitwise_and(place, 7)
            slots_of[k * 8 + n] = (j << 19) + ((first + slot * (BLK // HEAD)) << 7) + j
            n_of[k] = n + 1
            return carry

        lax.fori_loop(0, places[at, SLOTS], put, 0)


def chain_tile(c, step, odd):
    forward = 1 - 2 * jnp.bitwise_and(c, 1)
    return c - step * forward if odd else c + step * forward


def first_kernel(near, n_col, nb_rows, nb_cols, place_ref, *refs):
    own_ref, refs = refs[0], refs[1:]
    y_refs, refs = refs[: len(near) - 1], refs[len(near) - 1 :]
    x_refs, refs = refs[:2], refs[2:]
    acc, sums, y_blocks, slots_of, n_of, own_head, heads, places, todo, y_sems = refs
    r, c, l = place_ref[0], place_ref[1], place_ref[2]
    head_copy = pltpu.make_async_copy(own_ref.at[pl.ds(0, HEAD), :], own_head, y_sems.at[len(near)])
    head_copy.start()
    copies = []
    for at, (m, y_ref) in enumerate(zip(near, (own_ref, *y_refs))):
        copies.append(pltpu.make_async_copy(y_ref, tile_rows(y_blocks, jnp.bitwise_xor(r, m)), y_sems.at[at]))
        copies[-1].start()
    head_copy.wait()
    headers = [own_head[...]] + [ref[0:HEAD, :] for ref in (*y_refs, *x_refs)]
    read_headers(headers, heads, places)
    clear_blocks(acc)
    clear_blocks(sums)
    list_column(slots_of, n_of, places, list(enumerate(near)), r, nb_rows)
    for copy in copies:
        copy.wait()
    shares = [(c, l, 0, y_blocks, r * ROWS), (c, 1 - l, len(near), x_refs[0], 0)]
    shares.append((chain_tile(c, 1, False), l, len(near) + 1, x_refs[1], 0))
    for tile, layer, at, x_ref, x_base in shares:
        valid, first_inner = inner_of(n_col, nb_rows, nb_cols, tile, layer)
        n_slots = jnp.where(valid, places[at, SLOTS], 0)
        list_pairs(todo, 0, places, at, n_slots, first_inner, slots_of, n_of, nb_rows, nb_cols)
        multiply_pairs(todo, 0, x_ref, y_blocks, acc, sums, x_base)


def list_scratch(n_row, nb_rows, nb_cols, shares):
    return [
        pltpu.SMEM((n_row * nb_rows * 8,), jnp.int32),
        pltpu.SMEM((n_row * nb_rows,), jnp.int32),
        pltpu.VMEM((shares, BLK), jnp.int32),
        pltpu.SMEM((shares, BLK), jnp.int32),
        pltpu.SMEM((1, SLOTS * nb_cols + 1 + UNROLL), jnp.int32),
    ]


def multiply_first(place, near, ys, xs, n_row, n_col, nb_rows, nb_cols):
    shares = len(near) + len(xs)
    lists = list_scratch(n_row, nb_rows, nb_cols, shares)
    return pl.pallas_call(
        functools.partial(first_kernel, near, n_col, nb_rows, nb_cols),
        out_shape=[
            jax.ShapeDtypeStruct((nb_rows * nb_cols + 1, BLK, BLK), jnp.float32),
            jax.ShapeDtypeStruct((nb_cols + 1, 8, BLK), jnp.float32),
            jax.ShapeDtypeStruct((n_row * ROWS, BLK), jnp.bfloat16),
        ],
        in_specs=[SMEM, ANY] + [VMEM] * (shares - 1),
        out_specs=[VMEM] * 3,
        scratch_shapes=lists[:2]
        + [pltpu.VMEM((HEAD, BLK), jnp.bfloat16)]
        + lists[2:]
        + [pltpu.SemaphoreType.DMA((len(near) + 1,))],
        compiler_params=pltpu.CompilerParams(vmem_limit_bytes=24 * MIB),
        cost_estimate=SMALL,
        name="multiply_first",
    )(place, *[ys[m] for m in near], *xs)


def second_kernel(near, n_row, n_col, nb_rows, nb_cols, x_kinds, place_ref, *refs):
    distant = [m for m in range(n_row) if m not in near]
    y_refs, refs = refs[: len(distant)], refs[len(distant) :]
    x_refs, refs = refs[: len(x_kinds)], refs[len(x_kinds) :]
    half_refs, refs = refs[:2], refs[2:]
    acc, sums, y_blocks, slots_of, n_of, heads, places, todo, y_sems = refs[3:]
    r, c, l = place_ref[0], place_ref[1], place_ref[2]
    copies = []
    for at, (m, y_ref) in enumerate(zip(distant, y_refs)):
        copies.append(pltpu.make_async_copy(y_ref, tile_rows(y_blocks, jnp.bitwise_xor(r, m)), y_sems.at[at]))
        copies[-1].start()
    for copy in copies:
        copy.wait()
    headers = column_headers(y_blocks, r, n_row) + [ref[0:HEAD, :] for ref in (*x_refs, half_refs[0])]
    read_headers(headers, heads, places)
    list_column(slots_of, n_of, places, [(m, m) for m in range(n_row)], r, nb_rows)
    shares = [((0, False, False, True), 0, y_blocks, r * ROWS)]
    shares += [(kind, n_row + at, x_ref, 0) for at, (kind, x_ref) in enumerate(zip(x_kinds, x_refs))]
    for (step, odd, other, rest), at, x_ref, x_base in shares:
        tile = chain_tile(c, step, odd)
        valid, first_inner = inner_of(n_col, nb_rows, nb_cols, tile, 1 - l if other else l)
        if rest:
            for m in near:
                valid = jnp.logical_and(valid, jnp.bitwise_xor(tile, r) != m)
        n_slots = jnp.where(valid, places[at, SLOTS], 0)
        list_pairs(todo, 0, places, at, n_slots, first_inner, slots_of, n_of, nb_rows, nb_cols)
        multiply_pairs(todo, 0, x_ref, y_blocks, acc, sums, x_base)
    is_end = jnp.logical_or(c == 0, c == n_col - 1)
    step, at = n_col - 2, n_row + len(x_refs)
    tile = jnp.where(is_end, chain_tile(c, step, False), chain_tile(c, step, True))
    valid, first_inner = inner_of(n_col, nb_rows, nb_cols, tile, 1 - l)
    n_slots = jnp.where(valid, places[at, SLOTS], 0)
    for first_slot, end, x_ref, x_base in (
        (0, jnp.minimum(n_slots, HALF), half_refs[0], 0),
        (HALF, n_slots, half_refs[1], -FIRST_ROWS),
    ):
        list_pairs(todo, 0, places, at, end, first_inner, slots_of, n_of, nb_rows, nb_cols, first_slot)
        multiply_pairs(todo, 0, x_ref, y_blocks, acc, sums, x_base)


def multiply_second(place, near, ys, xs, x_kinds, halves, acc, sums, y_blocks, n_col, nb_rows, nb_cols):
    n_row = len(ys)
    distant = [ys[m] for m in range(n_row) if m not in near]
    operands = [place, *distant, *xs, *halves, acc, sums, y_blocks]
    lists = list_scratch(n_row, nb_rows, nb_cols, n_row + len(xs) + 1)
    return pl.pallas_call(
        functools.partial(second_kernel, near, n_row, n_col, nb_rows, nb_cols, x_kinds),
        out_shape=[jax.ShapeDtypeStruct(x.shape, x.dtype) for x in (acc, sums, y_blocks)]
        + [jax.ShapeDtypeStruct(x.shape, x.dtype) for x in lists[:2]],
        in_specs=[SMEM] + [ANY] * len(distant) + [VMEM] * (len(xs) + 5),
        out_specs=[VMEM] * 3 + [SMEM] * 2,
        input_output_aliases={len(operands) - 3 + at: at for at in range(3)},
        scratch_shapes=lists[2:] + [pltpu.SemaphoreType.DMA((len(distant),))],
        compiler_params=pltpu.CompilerParams(vmem_limit_bytes=24 * MIB),
        cost_estimate=SMALL,
        name="multiply_second",
    )(*operands)


def late_kernel(n_col, nb_rows, nb_cols, x_kinds, is_last, place_ref, slots_of, n_of, y_blocks, *refs):
    x_refs, refs = refs[: len(x_kinds)], refs[len(x_kinds) :]
    _, before_sums, acc = refs[:3]
    sums, heads, places, todo = refs[-4:]
    c, l = place_ref[1], place_ref[2]
    read_headers([ref[0:HEAD, :] for ref in x_refs], heads, places)
    for j in range(sums.shape[0]):
        sums[j] = before_sums[j]
    for at, (x_ref, (step, odd, other)) in enumerate(zip(x_refs, x_kinds)):
        valid, first_inner = inner_of(n_col, nb_rows, nb_cols, chain_tile(c, step, odd), 1 - l if other else l)
        n_slots = jnp.where(valid, places[at, SLOTS], 0)
        list_pairs(todo, 0, places, at, n_slots, first_inner, slots_of, n_of, nb_rows, nb_cols)
        multiply_pairs(todo, 0, x_ref, y_blocks, acc, sums)
    if is_last:
        totals = refs[3]
        totals[...] = jnp.zeros(totals.shape, totals.dtype)
        for j in range(nb_cols):
            totals[j : j + 1, :] = jnp.sum(sums[j], axis=0, keepdims=True)


def multiply_late(place, slots_of, n_of, y_blocks, xs, x_kinds, acc, sums, is_last, n_col, nb_rows, nb_cols):
    totals = jax.ShapeDtypeStruct((8, BLK), jnp.float32)
    same_sums = jax.ShapeDtypeStruct(sums.shape, sums.dtype)
    operands = [place, slots_of, n_of, y_blocks, *xs, acc, sums]
    return pl.pallas_call(
        functools.partial(late_kernel, n_col, nb_rows, nb_cols, x_kinds, is_last),
        out_shape=[jax.ShapeDtypeStruct(acc.shape, acc.dtype), totals if is_last else same_sums],
        in_specs=[SMEM] * 3 + [VMEM] * (len(operands) - 3),
        out_specs=[VMEM, VMEM],
        input_output_aliases={len(operands) - 2: 0},
        scratch_shapes=([pltpu.VMEM(sums.shape, jnp.float32)] if is_last else [])
        + list_scratch(0, nb_rows, nb_cols, len(xs))[2:],
        compiler_params=pltpu.CompilerParams(vmem_limit_bytes=24 * MIB),
        cost_estimate=SMALL,
        name="multiply_last" if is_last else "multiply_late",
    )(*operands)


def scale_kernel(scaling, nb_rows, nb_cols, *refs):
    product, sums = refs[0], refs[1:-3]
    out, scaled, sems = refs[-3:]
    total = sums[0][...]
    for other in sums[1:]:
        total = total + other[...]
    factor = scaling / total[0:nb_cols, :]

    def out_copy(i):
        rows = pl.ds(pl.multiple_of(i * BLK, BLK), BLK)
        return pltpu.make_async_copy(scaled.at[rows, :], out.at[rows, :], sems.at[i])

    def square(i, carry):
        for j in range(nb_cols):
            value = product[i * nb_cols + j]
            scaled[pl.ds(pl.multiple_of(i * BLK, BLK), BLK), j * BLK : (j + 1) * BLK] = (
                value * value * factor[j : j + 1, :]
            )
        out_copy(i).start()
        return carry

    lax.fori_loop(0, nb_rows, square, 0)

    def wait(i, carry):
        out_copy(i).wait()
        return carry

    lax.fori_loop(0, nb_rows, wait, 0)


def scale(product, sums, scaling, nb_rows, nb_cols):
    shape = (nb_rows * BLK, nb_cols * BLK)
    return pl.pallas_call(
        functools.partial(scale_kernel, scaling, nb_rows, nb_cols),
        out_shape=jax.ShapeDtypeStruct(shape, jnp.float32),
        in_specs=[VMEM] * (1 + len(sums)),
        out_specs=ANY,
        scratch_shapes=[pltpu.VMEM(shape, jnp.float32), pltpu.SemaphoreType.DMA((nb_rows,))],
        compiler_params=pltpu.CompilerParams(vmem_limit_bytes=16 * MIB),
        cost_estimate=pl.CostEstimate(flops=10**7, bytes_accessed=10 * 10**6, transcendentals=0),
        name="scale",
    )(product, *sums)


def even_tile(i, step):
    return i + step if i % 2 == 0 else i - step


def odd_tile(i, step):
    return i - step if i % 2 == 0 else i + step


def body(n_row, n_col, similarity, block_mask):
    nb_rows, nb_cols = block_mask.shape
    r, c, l = lax.axis_index("row"), lax.axis_index("col"), lax.axis_index("layer")
    place = jnp.stack([r, c, l]).astype(jnp.int32)
    mask = block_mask.T

    def hop(x, tile):
        targets = [tile(i, 1) if 0 <= tile(i, 1) < n_col else i for i in range(n_col)]
        return lax.ppermute(x, "col", list(enumerate(targets)))

    def sibling(x):
        return lax.ppermute(x, "layer", [(0, 1), (1, 0)])

    own = compact(mask, similarity)
    even = hop(own, even_tile)
    odd = hop(own, odd_tile)
    near = [m for m in range(n_row) if m.bit_count() <= 1]
    ys = [own] + [None] * (n_row - 1)
    for m in near[1:]:
        ys[m] = lax.ppermute(own, "row", [(s, s ^ m) for s in range(n_row)])
    for m in range(1, n_row):
        if ys[m] is None:
            bit = 1 << (m.bit_length() - 1)
            ys[m] = lax.ppermute(ys[m ^ bit], "row", [(s, s ^ bit) for s in range(n_row)])
    first_xs = [sibling(own), even]
    shares = [((0, False, True, True), first_xs[0]), ((1, True, False, False), odd), ((1, False, False, True), even)]
    first_xs[1], _ = lax.optimization_barrier((even, odd))
    acc, sums, y_blocks = multiply_first(place, near, ys, first_xs, n_row, n_col, nb_rows, nb_cols)
    for step in range(1, n_col - 2):
        shares.append(((step, True, True, False), sibling(odd)))
        shares.append(((step, False, True, False), sibling(even)))
        odd, even = hop(even, odd_tile), hop(odd, even_tile)
        shares += [((step + 1, True, False, False), odd), ((step + 1, False, False, False), even)]
    odd, sums = lax.optimization_barrier((odd, sums))
    last = hop(odd, even_tile)
    arrived = jnp.where(jnp.logical_or(c == 0, c == n_col - 1), even, odd)
    halves = [sibling(arrived[:FIRST_ROWS]), sibling(arrived[FIRST_ROWS:])]
    x_kinds, xs = zip(*shares)
    acc, sums, y_blocks, slots_of, n_of = multiply_second(
        place, near, ys, xs, x_kinds, halves, acc, sums, y_blocks, n_col, nb_rows, nb_cols
    )
    last, sums = lax.optimization_barrier((last, sums))
    other = sibling(last)
    kinds = [(n_col - 1, False, False)]
    sizes = n_col, nb_rows, nb_cols
    acc, sums = multiply_late(place, slots_of, n_of, y_blocks, [last], kinds, acc, sums, False, *sizes)
    kinds = [(n_col - 1, False, True)]
    product, sums = multiply_late(place, slots_of, n_of, y_blocks, [other], kinds, acc, sums, True, *sizes)
    all_sums = [sums]
    for m in range(1, n_row):
        all_sums.append(lax.ppermute(sums, "row", [(s, s ^ m) for s in range(n_row)]))
    return scale(product, all_sums, float(nb_rows * BLK * n_row), nb_rows, nb_cols)


def solution(mesh):
    n_row, n_col = mesh.shape["row"], mesh.shape["col"]
    return jax.shard_map(
        functools.partial(body, n_row, n_col),
        mesh=mesh,
        in_specs=(P("row", ("col", "layer")), P("row", ("col", "layer"))),
        out_specs=P("row", ("col", "layer")),
        check_vma=False,
    )
```

```python
import functools

import jax
import jax.numpy as jnp
from jax import lax
from jax.experimental import pallas as pl
from jax.experimental.pallas import tpu as pltpu
from jax.sharding import PartitionSpec as P

BLK = 128
SLOTS = 18
SHARE = SLOTS * BLK
HEAD = 16
HALF = 9
ROWS = HEAD + SHARE
FIRST_ROWS = HEAD + HALF * BLK
UNROLL = 8
LAG = 3
MIB = 1024 * 1024

SMEM = pl.BlockSpec(memory_space=pltpu.SMEM)
VMEM = pl.BlockSpec(memory_space=pltpu.VMEM)
ANY = pl.BlockSpec(memory_space=pl.ANY)
SMALL = pl.CostEstimate(flops=10**8, bytes_accessed=10**6, transcendentals=0)


def compact_kernel(mask_ref, sim_ref, out_ref, places, sems):
    nb_cols, nb_rows = mask_ref.shape

    def block_copy(slot, i, k):
        block = sim_ref.at[pl.ds(pl.multiple_of(i * BLK, BLK), BLK), pl.ds(k * BLK, BLK)]
        return pltpu.make_async_copy(
            block, out_ref.at[pl.ds(pl.multiple_of(HEAD + slot * BLK, HEAD), BLK), :], sems.at[slot]
        )

    def scan(i, count):
        for k in range(nb_cols):
            here = mask_ref[k, i]

            @pl.when(here != 0)
            def _():
                block_copy(count, i, k).start()
                places[count] = i * 8 + k

            count = count + here
        return count

    for slot in range(SLOTS):
        places[slot] = 0
    count = lax.fori_loop(0, nb_rows, scan, jnp.int32(0))
    lane = lax.broadcasted_iota(jnp.int32, (HEAD, BLK), 1)
    header = jnp.where(lane == SLOTS, count, 0)
    for slot in range(SLOTS):
        header = jnp.where(lane == slot, places[slot], header)
    out_ref[0:HEAD, :] = header.astype(jnp.float32).astype(out_ref.dtype)

    def wait(slot, carry):
        block_copy(slot, 0, 0).wait()
        return carry

    lax.fori_loop(0, count, wait, 0)


def compact(mask, similarity):
    return pl.pallas_call(
        compact_kernel,
        out_shape=pltpu.VMEM((ROWS, BLK), similarity.dtype),
        in_specs=[SMEM, ANY],
        out_specs=VMEM,
        scratch_shapes=[pltpu.SMEM((SLOTS,), jnp.int32), pltpu.SemaphoreType.DMA((SLOTS,))],
        cost_estimate=pl.CostEstimate(flops=0, bytes_accessed=2 * SHARE * BLK * 2, transcendentals=0),
        name="compact",
    )(mask, similarity)


def multiply_pairs(todo, share, x_ref, y_blocks, acc, sums, x_base=0):
    def multiply(step, carry):
        terms = []

        def add_term(packed, term):
            at = jnp.bitwise_and(packed, 127)
            j = jnp.bitwise_and(lax.shift_right_logical(packed, 19), 7)
            old = acc[at]
            new = old + term
            acc[at] = new
            sums[j] += jnp.sum((term * (old + new)).reshape(BLK // 8, 8, BLK), axis=0)

        for u in range(UNROLL):
            packed = todo[share, 1 + step * UNROLL + u]
            x = x_base + HEAD + lax.shift_right_logical(packed, 22) * BLK
            y = jnp.bitwise_and(lax.shift_right_logical(packed, 7), 4095) * HEAD
            x_block = x_ref[pl.ds(pl.multiple_of(x, HEAD), BLK), :]
            y_block = y_blocks[pl.ds(pl.multiple_of(y, HEAD), BLK), :]
            terms.append((packed, jnp.dot(x_block, y_block, preferred_element_type=jnp.float32)))
            if u >= LAG:
                add_term(*terms[u - LAG])
        for packed, term in terms[UNROLL - LAG :]:
            add_term(packed, term)
        return carry

    n_steps = lax.shift_right_logical(todo[share, 0] + UNROLL - 1, UNROLL.bit_length() - 1)
    lax.fori_loop(0, n_steps, multiply, 0)


def list_pairs(todo, share, places, at, n_slots, first_inner, slots_of, n_of, nb_rows, nb_cols, first_slot=0):
    def slot_pairs(slot, count):
        place = places[at, slot]
        k = first_inner + jnp.bitwise_and(place, 7)
        packed = (slot << 22) + lax.shift_right_logical(place, 3) * nb_cols

        n_pairs = n_of[k]

        def pair(n, carry):
            todo[share, 1 + count + n] = packed + slots_of[k * 8 + n]
            return carry

        pair(0, 0)
        pair(1, 0)
        lax.fori_loop(2, n_pairs, pair, 0)
        return count + n_pairs

    count = lax.fori_loop(first_slot, n_slots, slot_pairs, jnp.int32(0))
    for u in range(UNROLL):
        todo[share, 1 + count + u] = (first_slot << 22) + (nb_cols << 19) + nb_rows * nb_cols
    todo[share, 0] = count


def clear_blocks(ref):
    def clear(at, carry):
        ref[at] = jnp.zeros(ref.shape[1:], ref.dtype)
        return carry

    lax.fori_loop(0, ref.shape[0], clear, 0)


def read_headers(headers, heads, places):
    for at, header in enumerate(headers):
        heads[at : at + 1, :] = header.astype(jnp.float32)[0:1, :].astype(jnp.int32)
    for at in range(len(headers)):
        for slot in range(SLOTS + 1):
            places[at, slot] = heads[at, slot]


def inner_of(n_col, nb_rows, nb_cols, tile, layer):
    valid = jnp.logical_and(tile >= 0, tile < n_col)
    return valid, jnp.where(valid, tile, 0) * nb_rows + layer * nb_cols


def tile_rows(y_blocks, tile, rows=ROWS):
    return y_blocks.at[pl.ds(pl.multiple_of(tile * ROWS, HEAD), rows), :]


def column_headers(y_blocks, r, n_row):
    return [tile_rows(y_blocks, jnp.bitwise_xor(r, m), HEAD)[...] for m in range(n_row)]


def list_column(slots_of, n_of, places, sources, r, nb_rows):
    def no_slots(k, carry):
        n_of[k] = 0
        return carry

    lax.fori_loop(0, n_of.shape[0], no_slots, 0)
    for at, m in sources:
        tile = jnp.bitwise_xor(r, m)
        first = tile * (ROWS // HEAD) + 1

        def put(slot, carry):
            place = places[at, slot]
            k = tile * nb_rows + lax.shift_right_logical(place, 3)
            n = n_of[k]
            j = jnp.bitwise_and(place, 7)
            slots_of[k * 8 + n] = (j << 19) + ((first + slot * (BLK // HEAD)) << 7) + j
            n_of[k] = n + 1
            return carry

        lax.fori_loop(0, places[at, SLOTS], put, 0)


def chain_tile(c, step, odd):
    forward = 1 - 2 * jnp.bitwise_and(c, 1)
    return c - step * forward if odd else c + step * forward


def first_kernel(near, n_col, nb_rows, nb_cols, place_ref, *refs):
    own_ref, refs = refs[0], refs[1:]
    y_refs, refs = refs[: len(near) - 1], refs[len(near) - 1 :]
    x_refs, refs = refs[:2], refs[2:]
    acc, sums, y_blocks, slots_of, n_of, own_head, heads, places, todo, y_sems = refs
    r, c, l = place_ref[0], place_ref[1], place_ref[2]
    head_copy = pltpu.make_async_copy(own_ref.at[pl.ds(0, HEAD), :], own_head, y_sems.at[len(near)])
    head_copy.start()
    copies = []
    for at, (m, y_ref) in enumerate(zip(near, (own_ref, *y_refs))):
        copies.append(pltpu.make_async_copy(y_ref, tile_rows(y_blocks, jnp.bitwise_xor(r, m)), y_sems.at[at]))
        copies[-1].start()
    head_copy.wait()
    headers = [own_head[...]] + [ref[0:HEAD, :] for ref in (*y_refs, *x_refs)]
    read_headers(headers, heads, places)
    clear_blocks(acc)
    clear_blocks(sums)
    list_column(slots_of, n_of, places, list(enumerate(near)), r, nb_rows)
    for copy in copies:
        copy.wait()
    shares = [(c, l, 0, y_blocks, r * ROWS), (c, 1 - l, len(near), x_refs[0], 0)]
    shares.append((chain_tile(c, 1, False), l, len(near) + 1, x_refs[1], 0))
    for tile, layer, at, x_ref, x_base in shares:
        valid, first_inner = inner_of(n_col, nb_rows, nb_cols, tile, layer)
        n_slots = jnp.where(valid, places[at, SLOTS], 0)
        list_pairs(todo, 0, places, at, n_slots, first_inner, slots_of, n_of, nb_rows, nb_cols)
        multiply_pairs(todo, 0, x_ref, y_blocks, acc, sums, x_base)


def list_scratch(n_row, nb_rows, nb_cols, shares):
    return [
        pltpu.SMEM((n_row * nb_rows * 8,), jnp.int32),
        pltpu.SMEM((n_row * nb_rows,), jnp.int32),
        pltpu.VMEM((shares, BLK), jnp.int32),
        pltpu.SMEM((shares, BLK), jnp.int32),
        pltpu.SMEM((1, SLOTS * nb_cols + 1 + UNROLL), jnp.int32),
    ]


def multiply_first(place, near, ys, xs, n_row, n_col, nb_rows, nb_cols):
    shares = len(near) + len(xs)
    lists = list_scratch(n_row, nb_rows, nb_cols, shares)
    return pl.pallas_call(
        functools.partial(first_kernel, near, n_col, nb_rows, nb_cols),
        out_shape=[
            jax.ShapeDtypeStruct((nb_rows * nb_cols + 1, BLK, BLK), jnp.float32),
            jax.ShapeDtypeStruct((nb_cols + 1, 8, BLK), jnp.float32),
            jax.ShapeDtypeStruct((n_row * ROWS, BLK), jnp.bfloat16),
        ],
        in_specs=[SMEM, ANY] + [VMEM] * (shares - 1),
        out_specs=[VMEM] * 3,
        scratch_shapes=lists[:2]
        + [pltpu.VMEM((HEAD, BLK), jnp.bfloat16)]
        + lists[2:]
        + [pltpu.SemaphoreType.DMA((len(near) + 1,))],
        compiler_params=pltpu.CompilerParams(vmem_limit_bytes=24 * MIB),
        cost_estimate=SMALL,
        name="multiply_first",
    )(place, *[ys[m] for m in near], *xs)


def second_kernel(near, n_row, n_col, nb_rows, nb_cols, x_kinds, place_ref, *refs):
    distant = [m for m in range(n_row) if m not in near]
    y_refs, refs = refs[: len(distant)], refs[len(distant) :]
    x_refs, refs = refs[: len(x_kinds)], refs[len(x_kinds) :]
    half_refs, refs = refs[:2], refs[2:]
    acc, sums, y_blocks, slots_of, n_of, heads, places, todo, y_sems = refs[3:]
    r, c, l = place_ref[0], place_ref[1], place_ref[2]
    copies = []
    for at, (m, y_ref) in enumerate(zip(distant, y_refs)):
        copies.append(pltpu.make_async_copy(y_ref, tile_rows(y_blocks, jnp.bitwise_xor(r, m)), y_sems.at[at]))
        copies[-1].start()
    for copy in copies:
        copy.wait()
    headers = column_headers(y_blocks, r, n_row) + [ref[0:HEAD, :] for ref in (*x_refs, half_refs[0])]
    read_headers(headers, heads, places)
    list_column(slots_of, n_of, places, [(m, m) for m in range(n_row)], r, nb_rows)
    shares = [((0, False, False, True), 0, y_blocks, r * ROWS)]
    shares += [(kind, n_row + at, x_ref, 0) for at, (kind, x_ref) in enumerate(zip(x_kinds, x_refs))]
    for (step, odd, other, rest), at, x_ref, x_base in shares:
        tile = chain_tile(c, step, odd)
        valid, first_inner = inner_of(n_col, nb_rows, nb_cols, tile, 1 - l if other else l)
        if rest:
            for m in near:
                valid = jnp.logical_and(valid, jnp.bitwise_xor(tile, r) != m)
        n_slots = jnp.where(valid, places[at, SLOTS], 0)
        list_pairs(todo, 0, places, at, n_slots, first_inner, slots_of, n_of, nb_rows, nb_cols)
        multiply_pairs(todo, 0, x_ref, y_blocks, acc, sums, x_base)
    is_end = jnp.logical_or(c == 0, c == n_col - 1)
    step, at = n_col - 2, n_row + len(x_refs)
    tile = jnp.where(is_end, chain_tile(c, step, False), chain_tile(c, step, True))
    valid, first_inner = inner_of(n_col, nb_rows, nb_cols, tile, 1 - l)
    n_slots = jnp.where(valid, places[at, SLOTS], 0)
    for first_slot, end, x_ref, x_base in (
        (0, jnp.minimum(n_slots, HALF), half_refs[0], 0),
        (HALF, n_slots, half_refs[1], -FIRST_ROWS),
    ):
        list_pairs(todo, 0, places, at, end, first_inner, slots_of, n_of, nb_rows, nb_cols, first_slot)
        multiply_pairs(todo, 0, x_ref, y_blocks, acc, sums, x_base)


def multiply_second(place, near, ys, xs, x_kinds, halves, acc, sums, y_blocks, n_col, nb_rows, nb_cols):
    n_row = len(ys)
    distant = [ys[m] for m in range(n_row) if m not in near]
    operands = [place, *distant, *xs, *halves, acc, sums, y_blocks]
    lists = list_scratch(n_row, nb_rows, nb_cols, n_row + len(xs) + 1)
    return pl.pallas_call(
        functools.partial(second_kernel, near, n_row, n_col, nb_rows, nb_cols, x_kinds),
        out_shape=[jax.ShapeDtypeStruct(x.shape, x.dtype) for x in (acc, sums, y_blocks)]
        + [jax.ShapeDtypeStruct(x.shape, x.dtype) for x in lists[:2]],
        in_specs=[SMEM] + [ANY] * len(distant) + [VMEM] * (len(xs) + 5),
        out_specs=[VMEM] * 3 + [SMEM] * 2,
        input_output_aliases={len(operands) - 3 + at: at for at in range(3)},
        scratch_shapes=lists[2:] + [pltpu.SemaphoreType.DMA((len(distant),))],
        compiler_params=pltpu.CompilerParams(vmem_limit_bytes=24 * MIB),
        cost_estimate=SMALL,
        name="multiply_second",
    )(*operands)


def late_kernel(n_col, nb_rows, nb_cols, x_kinds, is_last, place_ref, slots_of, n_of, y_blocks, *refs):
    x_refs, refs = refs[: len(x_kinds)], refs[len(x_kinds) :]
    _, before_sums, acc = refs[:3]
    sums, heads, places, todo = refs[-4:]
    c, l = place_ref[1], place_ref[2]
    read_headers([ref[0:HEAD, :] for ref in x_refs], heads, places)
    for j in range(sums.shape[0]):
        sums[j] = before_sums[j]
    for at, (x_ref, (step, odd, other)) in enumerate(zip(x_refs, x_kinds)):
        valid, first_inner = inner_of(n_col, nb_rows, nb_cols, chain_tile(c, step, odd), 1 - l if other else l)
        n_slots = jnp.where(valid, places[at, SLOTS], 0)
        list_pairs(todo, 0, places, at, n_slots, first_inner, slots_of, n_of, nb_rows, nb_cols)
        multiply_pairs(todo, 0, x_ref, y_blocks, acc, sums)
    if is_last:
        totals = refs[3]
        totals[...] = jnp.zeros(totals.shape, totals.dtype)
        for j in range(nb_cols):
            totals[j : j + 1, :] = jnp.sum(sums[j], axis=0, keepdims=True)


def multiply_late(place, slots_of, n_of, y_blocks, xs, x_kinds, acc, sums, is_last, n_col, nb_rows, nb_cols):
    totals = jax.ShapeDtypeStruct((8, BLK), jnp.float32)
    same_sums = jax.ShapeDtypeStruct(sums.shape, sums.dtype)
    operands = [place, slots_of, n_of, y_blocks, *xs, acc, sums]
    return pl.pallas_call(
        functools.partial(late_kernel, n_col, nb_rows, nb_cols, x_kinds, is_last),
        out_shape=[jax.ShapeDtypeStruct(acc.shape, acc.dtype), totals if is_last else same_sums],
        in_specs=[SMEM] * 3 + [VMEM] * (len(operands) - 3),
        out_specs=[VMEM, VMEM],
        input_output_aliases={len(operands) - 2: 0},
        scratch_shapes=([pltpu.VMEM(sums.shape, jnp.float32)] if is_last else [])
        + list_scratch(0, nb_rows, nb_cols, len(xs))[2:],
        compiler_params=pltpu.CompilerParams(vmem_limit_bytes=24 * MIB),
        cost_estimate=SMALL,
        name="multiply_last" if is_last else "multiply_late",
    )(*operands)


def scale_kernel(scaling, nb_rows, nb_cols, *refs):
    product, sums, out, scaled, sems = refs
    total = sums[0]
    for other in range(1, sums.shape[0]):
        total = total + sums[other]
    factor = scaling / total[0:nb_cols, :]

    def out_copy(i):
        rows = pl.ds(pl.multiple_of(i * BLK, BLK), BLK)
        return pltpu.make_async_copy(scaled.at[rows, :], out.at[rows, :], sems.at[i])

    def square(i, carry):
        for j in range(nb_cols):
            value = product[i * nb_cols + j]
            scaled[pl.ds(pl.multiple_of(i * BLK, BLK), BLK), j * BLK : (j + 1) * BLK] = (
                value * value * factor[j : j + 1, :]
            )
        out_copy(i).start()
        return carry

    lax.fori_loop(0, nb_rows, square, 0)

    def wait(i, carry):
        out_copy(i).wait()
        return carry

    lax.fori_loop(0, nb_rows, wait, 0)


def scale(product, sums, scaling, nb_rows, nb_cols):
    shape = (nb_rows * BLK, nb_cols * BLK)
    return pl.pallas_call(
        functools.partial(scale_kernel, scaling, nb_rows, nb_cols),
        out_shape=jax.ShapeDtypeStruct(shape, jnp.float32),
        in_specs=[VMEM, VMEM],
        out_specs=ANY,
        scratch_shapes=[pltpu.VMEM(shape, jnp.float32), pltpu.SemaphoreType.DMA((nb_rows,))],
        compiler_params=pltpu.CompilerParams(vmem_limit_bytes=16 * MIB),
        cost_estimate=pl.CostEstimate(flops=10**7, bytes_accessed=10 * 10**6, transcendentals=0),
        name="scale",
    )(product, sums)


def even_tile(i, step):
    return i + step if i % 2 == 0 else i - step


def odd_tile(i, step):
    return i - step if i % 2 == 0 else i + step


def body(n_row, n_col, similarity, block_mask):
    nb_rows, nb_cols = block_mask.shape
    r, c, l = lax.axis_index("row"), lax.axis_index("col"), lax.axis_index("layer")
    place = jnp.stack([r, c, l]).astype(jnp.int32)
    mask = block_mask.T

    def hop(x, tile):
        targets = [tile(i, 1) if 0 <= tile(i, 1) < n_col else i for i in range(n_col)]
        return lax.ppermute(x, "col", list(enumerate(targets)))

    def sibling(x):
        return lax.ppermute(x, "layer", [(0, 1), (1, 0)])

    own = compact(mask, similarity)
    even = hop(own, even_tile)
    odd = hop(own, odd_tile)
    near = [m for m in range(n_row) if m.bit_count() <= 1]
    ys = [own] + [None] * (n_row - 1)
    for m in near[1:]:
        ys[m] = lax.ppermute(own, "row", [(s, s ^ m) for s in range(n_row)])
    for m in range(1, n_row):
        if ys[m] is None:
            bit = 1 << (m.bit_length() - 1)
            ys[m] = lax.ppermute(ys[m ^ bit], "row", [(s, s ^ bit) for s in range(n_row)])
    first_xs = [sibling(own), even]
    shares = [((0, False, True, True), first_xs[0]), ((1, True, False, False), odd), ((1, False, False, True), even)]
    first_xs[1], _ = lax.optimization_barrier((even, odd))
    acc, sums, y_blocks = multiply_first(place, near, ys, first_xs, n_row, n_col, nb_rows, nb_cols)
    for step in range(1, n_col - 2):
        shares.append(((step, True, True, False), sibling(odd)))
        shares.append(((step, False, True, False), sibling(even)))
        odd, even = hop(even, odd_tile), hop(odd, even_tile)
        shares += [((step + 1, True, False, False), odd), ((step + 1, False, False, False), even)]
    odd, sums = lax.optimization_barrier((odd, sums))
    last = hop(odd, even_tile)
    arrived = jnp.where(jnp.logical_or(c == 0, c == n_col - 1), even, odd)
    halves = [sibling(arrived[:FIRST_ROWS]), sibling(arrived[FIRST_ROWS:])]
    x_kinds, xs = zip(*shares)
    acc, sums, y_blocks, slots_of, n_of = multiply_second(
        place, near, ys, xs, x_kinds, halves, acc, sums, y_blocks, n_col, nb_rows, nb_cols
    )
    last, sums = lax.optimization_barrier((last, sums))
    other = sibling(last)
    kinds = [(n_col - 1, False, False)]
    sizes = n_col, nb_rows, nb_cols
    acc, sums = multiply_late(place, slots_of, n_of, y_blocks, [last], kinds, acc, sums, False, *sizes)
    kinds = [(n_col - 1, False, True)]
    product, sums = multiply_late(place, slots_of, n_of, y_blocks, [other], kinds, acc, sums, True, *sizes)
    all_sums = lax.all_gather(sums, "row", axis=0)
    return scale(product, all_sums, float(nb_rows * BLK * n_row), nb_rows, nb_cols)


def solution(mesh):
    n_row, n_col = mesh.shape["row"], mesh.shape["col"]
    return jax.shard_map(
        functools.partial(body, n_row, n_col),
        mesh=mesh,
        in_specs=(P("row", ("col", "layer")), P("row", ("col", "layer"))),
        out_specs=P("row", ("col", "layer")),
        check_vma=False,
    )
```

```python
import functools

import jax
import jax.numpy as jnp
from jax import lax
from jax.experimental import pallas as pl
from jax.experimental.pallas import tpu as pltpu
from jax.sharding import PartitionSpec as P

BLK = 128
SLOTS = 18
SHARE = SLOTS * BLK
HEAD = 16
HALF = 9
ROWS = HEAD + SHARE
FIRST_ROWS = HEAD + HALF * BLK
UNROLL = 8
LAG = 3
MIB = 1024 * 1024

SMEM = pl.BlockSpec(memory_space=pltpu.SMEM)
VMEM = pl.BlockSpec(memory_space=pltpu.VMEM)
ANY = pl.BlockSpec(memory_space=pl.ANY)
SMALL = pl.CostEstimate(flops=10**8, bytes_accessed=10**6, transcendentals=0)


def compact_kernel(mask_ref, sim_ref, out_ref, places, sems):
    nb_cols, nb_rows = mask_ref.shape

    def block_copy(slot, i, k):
        block = sim_ref.at[pl.ds(pl.multiple_of(i * BLK, BLK), BLK), pl.ds(k * BLK, BLK)]
        return pltpu.make_async_copy(
            block, out_ref.at[pl.ds(pl.multiple_of(HEAD + slot * BLK, HEAD), BLK), :], sems.at[slot]
        )

    def scan(i, count):
        for k in range(nb_cols):
            here = mask_ref[k, i]

            @pl.when(here != 0)
            def _():
                block_copy(count, i, k).start()
                places[count] = i * 8 + k

            count = count + here
        return count

    for slot in range(SLOTS):
        places[slot] = 0
    count = lax.fori_loop(0, nb_rows, scan, jnp.int32(0))
    lane = lax.broadcasted_iota(jnp.int32, (HEAD, BLK), 1)
    header = jnp.where(lane == SLOTS, count, 0)
    for slot in range(SLOTS):
        header = jnp.where(lane == slot, places[slot], header)
    out_ref[0:HEAD, :] = header.astype(jnp.float32).astype(out_ref.dtype)

    def wait(slot, carry):
        block_copy(slot, 0, 0).wait()
        return carry

    lax.fori_loop(0, count, wait, 0)


def compact(mask, similarity):
    return pl.pallas_call(
        compact_kernel,
        out_shape=pltpu.VMEM((ROWS, BLK), similarity.dtype),
        in_specs=[SMEM, ANY],
        out_specs=VMEM,
        scratch_shapes=[pltpu.SMEM((SLOTS,), jnp.int32), pltpu.SemaphoreType.DMA((SLOTS,))],
        cost_estimate=pl.CostEstimate(flops=0, bytes_accessed=2 * SHARE * BLK * 2, transcendentals=0),
        name="compact",
    )(mask, similarity)


def multiply_pairs(todo, share, x_ref, y_blocks, acc, sums, x_base=0):
    def multiply(step, carry):
        terms = []

        def add_term(packed, term):
            at = jnp.bitwise_and(packed, 127)
            j = jnp.bitwise_and(lax.shift_right_logical(packed, 19), 7)
            old = acc[at]
            new = old + term
            acc[at] = new
            sums[j] += jnp.sum((term * (old + new)).reshape(BLK // 8, 8, BLK), axis=0)

        for u in range(UNROLL):
            packed = todo[share, 1 + step * UNROLL + u]
            x = x_base + HEAD + lax.shift_right_logical(packed, 22) * BLK
            y = jnp.bitwise_and(lax.shift_right_logical(packed, 7), 4095) * HEAD
            x_block = x_ref[pl.ds(pl.multiple_of(x, HEAD), BLK), :]
            y_block = y_blocks[pl.ds(pl.multiple_of(y, HEAD), BLK), :]
            terms.append((packed, jnp.dot(x_block, y_block, preferred_element_type=jnp.float32)))
            if u >= LAG:
                add_term(*terms[u - LAG])
        for packed, term in terms[UNROLL - LAG :]:
            add_term(packed, term)
        return carry

    n_steps = lax.shift_right_logical(todo[share, 0] + UNROLL - 1, UNROLL.bit_length() - 1)
    lax.fori_loop(0, n_steps, multiply, 0)


def list_pairs(todo, share, places, at, n_slots, first_inner, slots_of, n_of, nb_rows, nb_cols, first_slot=0):
    def slot_pairs(slot, count):
        place = places[at, slot]
        k = first_inner + jnp.bitwise_and(place, 7)
        packed = (slot << 22) + lax.shift_right_logical(place, 3) * nb_cols

        n_pairs = n_of[k]

        def pair(n, carry):
            todo[share, 1 + count + n] = packed + slots_of[k * 8 + n]
            return carry

        pair(0, 0)
        pair(1, 0)
        lax.fori_loop(2, n_pairs, pair, 0)
        return count + n_pairs

    count = lax.fori_loop(first_slot, n_slots, slot_pairs, jnp.int32(0))
    for u in range(UNROLL):
        todo[share, 1 + count + u] = (first_slot << 22) + (nb_cols << 19) + nb_rows * nb_cols
    todo[share, 0] = count


def clear_blocks(ref):
    def clear(at, carry):
        ref[at] = jnp.zeros(ref.shape[1:], ref.dtype)
        return carry

    lax.fori_loop(0, ref.shape[0], clear, 0)


def read_headers(headers, heads, places):
    for at, header in enumerate(headers):
        heads[at : at + 1, :] = header.astype(jnp.float32)[0:1, :].astype(jnp.int32)
    for at in range(len(headers)):
        for slot in range(SLOTS + 1):
            places[at, slot] = heads[at, slot]


def inner_of(n_col, nb_rows, nb_cols, tile, layer):
    valid = jnp.logical_and(tile >= 0, tile < n_col)
    return valid, jnp.where(valid, tile, 0) * nb_rows + layer * nb_cols


def tile_rows(y_blocks, tile, rows=ROWS):
    return y_blocks.at[pl.ds(pl.multiple_of(tile * ROWS, HEAD), rows), :]


def column_headers(y_blocks, r, n_row):
    return [tile_rows(y_blocks, jnp.bitwise_xor(r, m), HEAD)[...] for m in range(n_row)]


def list_column(slots_of, n_of, places, sources, r, nb_rows):
    def no_slots(k, carry):
        n_of[k] = 0
        return carry

    lax.fori_loop(0, n_of.shape[0], no_slots, 0)
    for at, m in sources:
        tile = jnp.bitwise_xor(r, m)
        first = tile * (ROWS // HEAD) + 1

        def put(slot, carry):
            place = places[at, slot]
            k = tile * nb_rows + lax.shift_right_logical(place, 3)
            n = n_of[k]
            j = jnp.bitwise_and(place, 7)
            slots_of[k * 8 + n] = (j << 19) + ((first + slot * (BLK // HEAD)) << 7) + j
            n_of[k] = n + 1
            return carry

        lax.fori_loop(0, places[at, SLOTS], put, 0)


def chain_tile(c, step, odd):
    forward = 1 - 2 * jnp.bitwise_and(c, 1)
    return c - step * forward if odd else c + step * forward


def first_kernel(near, n_col, nb_rows, nb_cols, place_ref, *refs):
    own_ref, refs = refs[0], refs[1:]
    y_refs, refs = refs[: len(near) - 1], refs[len(near) - 1 :]
    x_refs, refs = refs[:2], refs[2:]
    acc, sums, y_blocks, slots_of, n_of, own_head, heads, places, todo, y_sems = refs
    r, c, l = place_ref[0], place_ref[1], place_ref[2]
    head_copy = pltpu.make_async_copy(own_ref.at[pl.ds(0, HEAD), :], own_head, y_sems.at[len(near)])
    head_copy.start()
    copies = []
    for at, (m, y_ref) in enumerate(zip(near, (own_ref, *y_refs))):
        copies.append(pltpu.make_async_copy(y_ref, tile_rows(y_blocks, jnp.bitwise_xor(r, m)), y_sems.at[at]))
        copies[-1].start()
    head_copy.wait()
    headers = [own_head[...]] + [ref[0:HEAD, :] for ref in (*y_refs, *x_refs)]
    read_headers(headers, heads, places)
    clear_blocks(acc)
    clear_blocks(sums)
    list_column(slots_of, n_of, places, list(enumerate(near)), r, nb_rows)
    for copy in copies:
        copy.wait()
    shares = [(c, l, 0, y_blocks, r * ROWS), (c, 1 - l, len(near), x_refs[0], 0)]
    shares.append((chain_tile(c, 1, False), l, len(near) + 1, x_refs[1], 0))
    for tile, layer, at, x_ref, x_base in shares:
        valid, first_inner = inner_of(n_col, nb_rows, nb_cols, tile, layer)
        n_slots = jnp.where(valid, places[at, SLOTS], 0)
        list_pairs(todo, 0, places, at, n_slots, first_inner, slots_of, n_of, nb_rows, nb_cols)
        multiply_pairs(todo, 0, x_ref, y_blocks, acc, sums, x_base)


def list_scratch(n_row, nb_rows, nb_cols, shares):
    return [
        pltpu.SMEM((n_row * nb_rows * 8,), jnp.int32),
        pltpu.SMEM((n_row * nb_rows,), jnp.int32),
        pltpu.VMEM((shares, BLK), jnp.int32),
        pltpu.SMEM((shares, BLK), jnp.int32),
        pltpu.SMEM((1, SLOTS * nb_cols + 1 + UNROLL), jnp.int32),
    ]


def multiply_first(place, near, ys, xs, n_row, n_col, nb_rows, nb_cols):
    shares = len(near) + len(xs)
    lists = list_scratch(n_row, nb_rows, nb_cols, shares)
    return pl.pallas_call(
        functools.partial(first_kernel, near, n_col, nb_rows, nb_cols),
        out_shape=[
            jax.ShapeDtypeStruct((nb_rows * nb_cols + 1, BLK, BLK), jnp.float32),
            jax.ShapeDtypeStruct((nb_cols + 1, 8, BLK), jnp.float32),
            jax.ShapeDtypeStruct((n_row * ROWS, BLK), jnp.bfloat16),
        ],
        in_specs=[SMEM, ANY] + [VMEM] * (shares - 1),
        out_specs=[VMEM] * 3,
        scratch_shapes=lists[:2]
        + [pltpu.VMEM((HEAD, BLK), jnp.bfloat16)]
        + lists[2:]
        + [pltpu.SemaphoreType.DMA((len(near) + 1,))],
        compiler_params=pltpu.CompilerParams(vmem_limit_bytes=24 * MIB),
        cost_estimate=SMALL,
        name="multiply_first",
    )(place, *[ys[m] for m in near], *xs)


def second_kernel(near, n_row, n_col, nb_rows, nb_cols, x_kinds, place_ref, *refs):
    distant = [m for m in range(n_row) if m not in near]
    y_refs, refs = refs[: len(distant)], refs[len(distant) :]
    x_refs, refs = refs[: len(x_kinds)], refs[len(x_kinds) :]
    half_refs, refs = refs[:2], refs[2:]
    acc, sums, y_blocks, slots_of, n_of, heads, places, todo, y_sems = refs[3:]
    r, c, l = place_ref[0], place_ref[1], place_ref[2]
    copies = []
    for at, (m, y_ref) in enumerate(zip(distant, y_refs)):
        copies.append(pltpu.make_async_copy(y_ref, tile_rows(y_blocks, jnp.bitwise_xor(r, m)), y_sems.at[at]))
        copies[-1].start()
    for copy in copies:
        copy.wait()
    headers = column_headers(y_blocks, r, n_row) + [ref[0:HEAD, :] for ref in (*x_refs, half_refs[0])]
    read_headers(headers, heads, places)
    list_column(slots_of, n_of, places, [(m, m) for m in range(n_row)], r, nb_rows)
    shares = [((0, False, False, True), 0, y_blocks, r * ROWS)]
    shares += [(kind, n_row + at, x_ref, 0) for at, (kind, x_ref) in enumerate(zip(x_kinds, x_refs))]
    for (step, odd, other, rest), at, x_ref, x_base in shares:
        tile = chain_tile(c, step, odd)
        valid, first_inner = inner_of(n_col, nb_rows, nb_cols, tile, 1 - l if other else l)
        if rest:
            for m in near:
                valid = jnp.logical_and(valid, jnp.bitwise_xor(tile, r) != m)
        n_slots = jnp.where(valid, places[at, SLOTS], 0)
        list_pairs(todo, 0, places, at, n_slots, first_inner, slots_of, n_of, nb_rows, nb_cols)
        multiply_pairs(todo, 0, x_ref, y_blocks, acc, sums, x_base)
    is_end = jnp.logical_or(c == 0, c == n_col - 1)
    step, at = n_col - 2, n_row + len(x_refs)
    tile = jnp.where(is_end, chain_tile(c, step, False), chain_tile(c, step, True))
    valid, first_inner = inner_of(n_col, nb_rows, nb_cols, tile, 1 - l)
    n_slots = jnp.where(valid, places[at, SLOTS], 0)
    for first_slot, end, x_ref, x_base in (
        (0, jnp.minimum(n_slots, HALF), half_refs[0], 0),
        (HALF, n_slots, half_refs[1], -FIRST_ROWS),
    ):
        list_pairs(todo, 0, places, at, end, first_inner, slots_of, n_of, nb_rows, nb_cols, first_slot)
        multiply_pairs(todo, 0, x_ref, y_blocks, acc, sums, x_base)


def multiply_second(place, near, ys, xs, x_kinds, halves, acc, sums, y_blocks, n_col, nb_rows, nb_cols):
    n_row = len(ys)
    distant = [ys[m] for m in range(n_row) if m not in near]
    operands = [place, *distant, *xs, *halves, acc, sums, y_blocks]
    lists = list_scratch(n_row, nb_rows, nb_cols, n_row + len(xs) + 1)
    return pl.pallas_call(
        functools.partial(second_kernel, near, n_row, n_col, nb_rows, nb_cols, x_kinds),
        out_shape=[jax.ShapeDtypeStruct(x.shape, x.dtype) for x in (acc, sums, y_blocks)]
        + [jax.ShapeDtypeStruct(x.shape, x.dtype) for x in lists[:2]],
        in_specs=[SMEM] + [ANY] * len(distant) + [VMEM] * (len(xs) + 5),
        out_specs=[VMEM] * 3 + [SMEM] * 2,
        input_output_aliases={len(operands) - 3 + at: at for at in range(3)},
        scratch_shapes=lists[2:] + [pltpu.SemaphoreType.DMA((len(distant),))],
        compiler_params=pltpu.CompilerParams(vmem_limit_bytes=24 * MIB),
        cost_estimate=SMALL,
        name="multiply_second",
    )(*operands)


def late_kernel(n_col, nb_rows, nb_cols, x_kinds, is_last, place_ref, slots_of, n_of, y_blocks, *refs):
    x_refs, refs = refs[: len(x_kinds)], refs[len(x_kinds) :]
    _, before_sums, acc = refs[:3]
    sums, heads, places, todo = refs[-4:]
    c, l = place_ref[1], place_ref[2]
    read_headers([ref[0:HEAD, :] for ref in x_refs], heads, places)
    for j in range(sums.shape[0]):
        sums[j] = before_sums[j]
    for at, (x_ref, (step, odd, other)) in enumerate(zip(x_refs, x_kinds)):
        valid, first_inner = inner_of(n_col, nb_rows, nb_cols, chain_tile(c, step, odd), 1 - l if other else l)
        n_slots = jnp.where(valid, places[at, SLOTS], 0)
        list_pairs(todo, 0, places, at, n_slots, first_inner, slots_of, n_of, nb_rows, nb_cols)
        multiply_pairs(todo, 0, x_ref, y_blocks, acc, sums)
    if is_last:
        totals = refs[3]
        totals[...] = jnp.zeros(totals.shape, totals.dtype)
        for j in range(nb_cols):
            totals[j : j + 1, :] = jnp.sum(sums[j], axis=0, keepdims=True)


def multiply_late(place, slots_of, n_of, y_blocks, xs, x_kinds, acc, sums, is_last, n_col, nb_rows, nb_cols):
    totals = jax.ShapeDtypeStruct((8, BLK), jnp.float32)
    same_sums = jax.ShapeDtypeStruct(sums.shape, sums.dtype)
    operands = [place, slots_of, n_of, y_blocks, *xs, acc, sums]
    return pl.pallas_call(
        functools.partial(late_kernel, n_col, nb_rows, nb_cols, x_kinds, is_last),
        out_shape=[jax.ShapeDtypeStruct(acc.shape, acc.dtype), totals if is_last else same_sums],
        in_specs=[SMEM] * 3 + [VMEM] * (len(operands) - 3),
        out_specs=[VMEM, VMEM],
        input_output_aliases={len(operands) - 2: 0},
        scratch_shapes=([pltpu.VMEM(sums.shape, jnp.float32)] if is_last else [])
        + list_scratch(0, nb_rows, nb_cols, len(xs))[2:],
        compiler_params=pltpu.CompilerParams(vmem_limit_bytes=24 * MIB),
        cost_estimate=SMALL,
        name="multiply_last" if is_last else "multiply_late",
    )(*operands)


def scale_kernel(scaling, nb_rows, nb_cols, *refs):
    product, sums = refs[0], refs[1:-3]
    out, scaled, sems = refs[-3:]
    total = sums[0][...]
    for other in sums[1:]:
        total = total + other[...]
    factor = scaling / total[0:nb_cols, :]

    def out_copy(i):
        rows = pl.ds(pl.multiple_of(i * BLK, BLK), BLK)
        return pltpu.make_async_copy(scaled.at[rows, :], out.at[rows, :], sems.at[i])

    def square(i, carry):
        for j in range(nb_cols):
            value = product[i * nb_cols + j]
            scaled[pl.ds(pl.multiple_of(i * BLK, BLK), BLK), j * BLK : (j + 1) * BLK] = (
                value * value * factor[j : j + 1, :]
            )
        out_copy(i).start()
        return carry

    lax.fori_loop(0, nb_rows, square, 0)

    def wait(i, carry):
        out_copy(i).wait()
        return carry

    lax.fori_loop(0, nb_rows, wait, 0)


def scale(product, sums, scaling, nb_rows, nb_cols):
    shape = (nb_rows * BLK, nb_cols * BLK)
    return pl.pallas_call(
        functools.partial(scale_kernel, scaling, nb_rows, nb_cols),
        out_shape=jax.ShapeDtypeStruct(shape, jnp.float32),
        in_specs=[VMEM] * (1 + len(sums)),
        out_specs=ANY,
        scratch_shapes=[pltpu.VMEM(shape, jnp.float32), pltpu.SemaphoreType.DMA((nb_rows,))],
        compiler_params=pltpu.CompilerParams(vmem_limit_bytes=16 * MIB),
        cost_estimate=pl.CostEstimate(flops=10**7, bytes_accessed=10 * 10**6, transcendentals=0),
        name="scale",
    )(product, *sums)


def even_tile(i, step):
    return i + step if i % 2 == 0 else i - step


def odd_tile(i, step):
    return i - step if i % 2 == 0 else i + step


def body(n_row, n_col, similarity, block_mask):
    nb_rows, nb_cols = block_mask.shape
    r, c, l = lax.axis_index("row"), lax.axis_index("col"), lax.axis_index("layer")
    place = jnp.stack([r, c, l]).astype(jnp.int32)
    mask = block_mask.T

    def hop(x, tile):
        pairs = []
        for i in range(n_col):
            partner = tile(i, 1)
            for layer in range(2):
                if 0 <= partner < n_col:
                    pairs.append((2 * i + layer, 2 * partner + layer))
                else:
                    pairs.append((2 * i + layer, 2 * i + 1 - layer))
        return lax.ppermute(x, ("col", "layer"), pairs)

    def sibling(x):
        return lax.ppermute(x, "layer", [(0, 1), (1, 0)])

    own = compact(mask, similarity)
    even = hop(own, even_tile)
    odd = hop(own, odd_tile)
    near = [m for m in range(n_row) if m.bit_count() <= 1]
    ys = [own] + [None] * (n_row - 1)
    for m in near[1:]:
        ys[m] = lax.ppermute(own, "row", [(s, s ^ m) for s in range(n_row)])
    for m in range(1, n_row):
        if ys[m] is None:
            bit = 1 << (m.bit_length() - 1)
            ys[m] = lax.ppermute(ys[m ^ bit], "row", [(s, s ^ bit) for s in range(n_row)])
    first_xs = [sibling(own), even]
    shares = [((0, False, True, True), first_xs[0]), ((1, True, False, False), odd), ((1, False, False, True), even)]
    first_xs[1], _ = lax.optimization_barrier((even, odd))
    acc, sums, y_blocks = multiply_first(place, near, ys, first_xs, n_row, n_col, nb_rows, nb_cols)
    for step in range(1, n_col - 2):
        shares.append(((step, True, True, False), sibling(odd)))
        shares.append(((step, False, True, False), sibling(even)))
        odd, even = hop(even, odd_tile), hop(odd, even_tile)
        shares += [((step + 1, True, False, False), odd), ((step + 1, False, False, False), even)]
    odd, sums = lax.optimization_barrier((odd, sums))
    last = hop(odd, even_tile)
    arrived = jnp.where(jnp.logical_or(c == 0, c == n_col - 1), even, odd)
    halves = [sibling(arrived[:FIRST_ROWS]), sibling(arrived[FIRST_ROWS:])]
    x_kinds, xs = zip(*shares)
    acc, sums, y_blocks, slots_of, n_of = multiply_second(
        place, near, ys, xs, x_kinds, halves, acc, sums, y_blocks, n_col, nb_rows, nb_cols
    )
    last, sums = lax.optimization_barrier((last, sums))
    other = sibling(last)
    kinds = [(n_col - 1, False, False)]
    sizes = n_col, nb_rows, nb_cols
    acc, sums = multiply_late(place, slots_of, n_of, y_blocks, [last], kinds, acc, sums, False, *sizes)
    kinds = [(n_col - 1, False, True)]
    product, sums = multiply_late(place, slots_of, n_of, y_blocks, [other], kinds, acc, sums, True, *sizes)
    all_sums = [sums]
    for m in range(1, n_row):
        all_sums.append(lax.ppermute(sums, "row", [(s, s ^ m) for s in range(n_row)]))
    return scale(product, all_sums, float(nb_rows * BLK * n_row), nb_rows, nb_cols)


def solution(mesh):
    n_row, n_col = mesh.shape["row"], mesh.shape["col"]
    return jax.shard_map(
        functools.partial(body, n_row, n_col),
        mesh=mesh,
        in_specs=(P("row", ("col", "layer")), P("row", ("col", "layer"))),
        out_specs=P("row", ("col", "layer")),
        check_vma=False,
    )
```

```python
import functools

import jax
import jax.numpy as jnp
from jax import lax
from jax.experimental import pallas as pl
from jax.experimental.pallas import tpu as pltpu
from jax.sharding import PartitionSpec as P

BLK = 128
SLOTS = 18
SHARE = SLOTS * BLK
HEAD = 16
HALF = 9
ROWS = HEAD + SHARE
FIRST_ROWS = HEAD + HALF * BLK
UNROLL = 8
LAG = 3
MIB = 1024 * 1024

SMEM = pl.BlockSpec(memory_space=pltpu.SMEM)
VMEM = pl.BlockSpec(memory_space=pltpu.VMEM)
ANY = pl.BlockSpec(memory_space=pl.ANY)
SMALL = pl.CostEstimate(flops=10**8, bytes_accessed=10**6, transcendentals=0)


def compact_kernel(mask_ref, sim_ref, out_ref, places, sems):
    nb_cols, nb_rows = mask_ref.shape

    def block_copy(slot, i, k):
        block = sim_ref.at[pl.ds(pl.multiple_of(i * BLK, BLK), BLK), pl.ds(k * BLK, BLK)]
        return pltpu.make_async_copy(
            block, out_ref.at[pl.ds(pl.multiple_of(HEAD + slot * BLK, HEAD), BLK), :], sems.at[slot]
        )

    def scan(i, count):
        for k in range(nb_cols):
            here = mask_ref[k, i]

            @pl.when(here != 0)
            def _():
                block_copy(count, i, k).start()
                places[count] = i * 8 + k

            count = count + here
        return count

    for slot in range(SLOTS):
        places[slot] = 0
    count = lax.fori_loop(0, nb_rows, scan, jnp.int32(0))
    lane = lax.broadcasted_iota(jnp.int32, (HEAD, BLK), 1)
    header = jnp.where(lane == SLOTS, count, 0)
    for slot in range(SLOTS):
        header = jnp.where(lane == slot, places[slot], header)
    out_ref[0:HEAD, :] = header.astype(jnp.float32).astype(out_ref.dtype)

    def wait(slot, carry):
        block_copy(slot, 0, 0).wait()
        return carry

    lax.fori_loop(0, count, wait, 0)


def compact(mask, similarity):
    return pl.pallas_call(
        compact_kernel,
        out_shape=pltpu.VMEM((ROWS, BLK), similarity.dtype),
        in_specs=[SMEM, ANY],
        out_specs=VMEM,
        scratch_shapes=[pltpu.SMEM((SLOTS,), jnp.int32), pltpu.SemaphoreType.DMA((SLOTS,))],
        cost_estimate=pl.CostEstimate(flops=0, bytes_accessed=2 * SHARE * BLK * 2, transcendentals=0),
        name="compact",
    )(mask, similarity)


def multiply_pairs(todo, share, x_ref, y_blocks, acc, sums, x_base=0):
    def multiply(step, carry):
        terms = []

        def add_term(packed, term):
            at = jnp.bitwise_and(packed, 127)
            j = jnp.bitwise_and(lax.shift_right_logical(packed, 19), 7)
            old = acc[at]
            new = old + term
            acc[at] = new
            sums[j] += jnp.sum((term * (old + new)).reshape(BLK // 8, 8, BLK), axis=0)

        for u in range(UNROLL):
            packed = todo[share, 1 + step * UNROLL + u]
            x = x_base + HEAD + lax.shift_right_logical(packed, 22) * BLK
            y = jnp.bitwise_and(lax.shift_right_logical(packed, 7), 4095) * HEAD
            x_block = x_ref[pl.ds(pl.multiple_of(x, HEAD), BLK), :]
            y_block = y_blocks[pl.ds(pl.multiple_of(y, HEAD), BLK), :]
            terms.append((packed, jnp.dot(x_block, y_block, preferred_element_type=jnp.float32)))
            if u >= LAG:
                add_term(*terms[u - LAG])
        for packed, term in terms[UNROLL - LAG :]:
            add_term(packed, term)
        return carry

    n_steps = lax.shift_right_logical(todo[share, 0] + UNROLL - 1, UNROLL.bit_length() - 1)
    lax.fori_loop(0, n_steps, multiply, 0)


def list_pairs(todo, share, places, at, n_slots, first_inner, slots_of, n_of, nb_rows, nb_cols, first_slot=0):
    def slot_pairs(slot, count):
        place = places[at, slot]
        k = first_inner + jnp.bitwise_and(place, 7)
        packed = (slot << 22) + lax.shift_right_logical(place, 3) * nb_cols

        n_pairs = n_of[k]

        def pair(n, carry):
            todo[share, 1 + count + n] = packed + slots_of[k * 8 + n]
            return carry

        pair(0, 0)
        pair(1, 0)
        lax.fori_loop(2, n_pairs, pair, 0)
        return count + n_pairs

    count = lax.fori_loop(first_slot, n_slots, slot_pairs, jnp.int32(0))
    for u in range(UNROLL):
        todo[share, 1 + count + u] = (first_slot << 22) + (nb_cols << 19) + nb_rows * nb_cols
    todo[share, 0] = count


def clear_blocks(ref):
    def clear(at, carry):
        ref[at] = jnp.zeros(ref.shape[1:], ref.dtype)
        return carry

    lax.fori_loop(0, ref.shape[0], clear, 0)


def read_headers(headers, heads, places):
    for at, header in enumerate(headers):
        heads[at : at + 1, :] = header.astype(jnp.float32)[0:1, :].astype(jnp.int32)
    for at in range(len(headers)):
        for slot in range(SLOTS + 1):
            places[at, slot] = heads[at, slot]


def inner_of(n_col, nb_rows, nb_cols, tile, layer):
    valid = jnp.logical_and(tile >= 0, tile < n_col)
    return valid, jnp.where(valid, tile, 0) * nb_rows + layer * nb_cols


def tile_rows(y_blocks, tile, rows=ROWS):
    return y_blocks.at[pl.ds(pl.multiple_of(tile * ROWS, HEAD), rows), :]


def column_headers(y_blocks, r, n_row):
    return [tile_rows(y_blocks, jnp.bitwise_xor(r, m), HEAD)[...] for m in range(n_row)]


def list_column(slots_of, n_of, places, sources, r, nb_rows):
    def no_slots(k, carry):
        n_of[k] = 0
        return carry

    lax.fori_loop(0, n_of.shape[0], no_slots, 0)
    for at, m in sources:
        tile = jnp.bitwise_xor(r, m)
        first = tile * (ROWS // HEAD) + 1

        def put(slot, carry):
            place = places[at, slot]
            k = tile * nb_rows + lax.shift_right_logical(place, 3)
            n = n_of[k]
            j = jnp.bitwise_and(place, 7)
            slots_of[k * 8 + n] = (j << 19) + ((first + slot * (BLK // HEAD)) << 7) + j
            n_of[k] = n + 1
            return carry

        lax.fori_loop(0, places[at, SLOTS], put, 0)


def chain_tile(c, step, odd):
    forward = 1 - 2 * jnp.bitwise_and(c, 1)
    return c - step * forward if odd else c + step * forward


def first_kernel(near, n_col, nb_rows, nb_cols, place_ref, *refs):
    own_ref, refs = refs[0], refs[1:]
    y_refs, refs = refs[: len(near) - 1], refs[len(near) - 1 :]
    x_refs, refs = refs[:3], refs[3:]
    acc, sums, y_blocks, slots_of, n_of, own_head, heads, places, todo, y_sems = refs
    r, c, l = place_ref[0], place_ref[1], place_ref[2]
    head_copy = pltpu.make_async_copy(own_ref.at[pl.ds(0, HEAD), :], own_head, y_sems.at[len(near)])
    head_copy.start()
    copies = []
    for at, (m, y_ref) in enumerate(zip(near, (own_ref, *y_refs))):
        copies.append(pltpu.make_async_copy(y_ref, tile_rows(y_blocks, jnp.bitwise_xor(r, m)), y_sems.at[at]))
        copies[-1].start()
    head_copy.wait()
    headers = [own_head[...]] + [ref[0:HEAD, :] for ref in (*y_refs, *x_refs)]
    read_headers(headers, heads, places)
    clear_blocks(acc)
    clear_blocks(sums)
    list_column(slots_of, n_of, places, list(enumerate(near)), r, nb_rows)
    for copy in copies:
        copy.wait()
    shares = [(c, l, 0, y_blocks, r * ROWS), (c, 1 - l, len(near), x_refs[0], 0)]
    shares.append((chain_tile(c, 1, True), l, len(near) + 1, x_refs[1], 0))
    shares.append((chain_tile(c, 1, False), l, len(near) + 2, x_refs[2], 0))
    for tile, layer, at, x_ref, x_base in shares:
        valid, first_inner = inner_of(n_col, nb_rows, nb_cols, tile, layer)
        n_slots = jnp.where(valid, places[at, SLOTS], 0)
        list_pairs(todo, 0, places, at, n_slots, first_inner, slots_of, n_of, nb_rows, nb_cols)
        multiply_pairs(todo, 0, x_ref, y_blocks, acc, sums, x_base)


def list_scratch(n_row, nb_rows, nb_cols, shares):
    return [
        pltpu.SMEM((n_row * nb_rows * 8,), jnp.int32),
        pltpu.SMEM((n_row * nb_rows,), jnp.int32),
        pltpu.VMEM((shares, BLK), jnp.int32),
        pltpu.SMEM((shares, BLK), jnp.int32),
        pltpu.SMEM((1, SLOTS * nb_cols + 1 + UNROLL), jnp.int32),
    ]


def multiply_first(place, near, ys, xs, n_row, n_col, nb_rows, nb_cols):
    shares = len(near) + len(xs)
    lists = list_scratch(n_row, nb_rows, nb_cols, shares)
    return pl.pallas_call(
        functools.partial(first_kernel, near, n_col, nb_rows, nb_cols),
        out_shape=[
            jax.ShapeDtypeStruct((nb_rows * nb_cols + 1, BLK, BLK), jnp.float32),
            jax.ShapeDtypeStruct((nb_cols + 1, 8, BLK), jnp.float32),
            jax.ShapeDtypeStruct((n_row * ROWS, BLK), jnp.bfloat16),
        ],
        in_specs=[SMEM] + [VMEM] * shares,
        out_specs=[VMEM] * 3,
        scratch_shapes=lists[:2]
        + [pltpu.VMEM((HEAD, BLK), jnp.bfloat16)]
        + lists[2:]
        + [pltpu.SemaphoreType.DMA((len(near) + 1,))],
        compiler_params=pltpu.CompilerParams(vmem_limit_bytes=8 * MIB),
        cost_estimate=SMALL,
        name="multiply_first",
    )(place, *[ys[m] for m in near], *xs)


def second_kernel(near, n_row, n_col, nb_rows, nb_cols, x_kinds, place_ref, *refs):
    distant = [m for m in range(n_row) if m not in near]
    y_refs, refs = refs[: len(distant)], refs[len(distant) :]
    x_refs, refs = refs[: len(x_kinds)], refs[len(x_kinds) :]
    half_refs, refs = refs[:2], refs[2:]
    acc, sums, y_blocks, slots_of, n_of, heads, places, todo, y_sems = refs[3:]
    r, c, l = place_ref[0], place_ref[1], place_ref[2]
    copies = []
    for at, (m, y_ref) in enumerate(zip(distant, y_refs)):
        copies.append(pltpu.make_async_copy(y_ref, tile_rows(y_blocks, jnp.bitwise_xor(r, m)), y_sems.at[at]))
        copies[-1].start()
    for copy in copies:
        copy.wait()
    headers = column_headers(y_blocks, r, n_row) + [ref[0:HEAD, :] for ref in (*x_refs, half_refs[0])]
    read_headers(headers, heads, places)
    list_column(slots_of, n_of, places, [(m, m) for m in range(n_row)], r, nb_rows)
    shares = [((0, False, False, True), 0, y_blocks, r * ROWS)]
    shares += [(kind, n_row + at, x_ref, 0) for at, (kind, x_ref) in enumerate(zip(x_kinds, x_refs))]
    for (step, odd, other, rest), at, x_ref, x_base in shares:
        tile = chain_tile(c, step, odd)
        valid, first_inner = inner_of(n_col, nb_rows, nb_cols, tile, 1 - l if other else l)
        if rest:
            for m in near:
                valid = jnp.logical_and(valid, jnp.bitwise_xor(tile, r) != m)
        n_slots = jnp.where(valid, places[at, SLOTS], 0)
        list_pairs(todo, 0, places, at, n_slots, first_inner, slots_of, n_of, nb_rows, nb_cols)
        multiply_pairs(todo, 0, x_ref, y_blocks, acc, sums, x_base)
    is_end = jnp.logical_or(c == 0, c == n_col - 1)
    step, at = n_col - 2, n_row + len(x_refs)
    tile = jnp.where(is_end, chain_tile(c, step, False), chain_tile(c, step, True))
    valid, first_inner = inner_of(n_col, nb_rows, nb_cols, tile, 1 - l)
    n_slots = jnp.where(valid, places[at, SLOTS], 0)
    for first_slot, end, x_ref, x_base in (
        (0, jnp.minimum(n_slots, HALF), half_refs[0], 0),
        (HALF, n_slots, half_refs[1], -FIRST_ROWS),
    ):
        list_pairs(todo, 0, places, at, end, first_inner, slots_of, n_of, nb_rows, nb_cols, first_slot)
        multiply_pairs(todo, 0, x_ref, y_blocks, acc, sums, x_base)


def multiply_second(place, near, ys, xs, x_kinds, halves, acc, sums, y_blocks, n_col, nb_rows, nb_cols):
    n_row = len(ys)
    distant = [ys[m] for m in range(n_row) if m not in near]
    operands = [place, *distant, *xs, *halves, acc, sums, y_blocks]
    lists = list_scratch(n_row, nb_rows, nb_cols, n_row + len(xs) + 1)
    return pl.pallas_call(
        functools.partial(second_kernel, near, n_row, n_col, nb_rows, nb_cols, x_kinds),
        out_shape=[jax.ShapeDtypeStruct(x.shape, x.dtype) for x in (acc, sums, y_blocks)]
        + [jax.ShapeDtypeStruct(x.shape, x.dtype) for x in lists[:2]],
        in_specs=[SMEM] + [ANY] * len(distant) + [VMEM] * (len(xs) + 5),
        out_specs=[VMEM] * 3 + [SMEM] * 2,
        input_output_aliases={len(operands) - 3 + at: at for at in range(3)},
        scratch_shapes=lists[2:] + [pltpu.SemaphoreType.DMA((len(distant),))],
        compiler_params=pltpu.CompilerParams(vmem_limit_bytes=8 * MIB),
        cost_estimate=SMALL,
        name="multiply_second",
    )(*operands)


def late_kernel(n_col, nb_rows, nb_cols, x_kinds, is_last, place_ref, slots_of, n_of, y_blocks, *refs):
    x_refs, refs = refs[: len(x_kinds)], refs[len(x_kinds) :]
    _, before_sums, acc = refs[:3]
    sums, heads, places, todo = refs[-4:]
    c, l = place_ref[1], place_ref[2]
    read_headers([ref[0:HEAD, :] for ref in x_refs], heads, places)
    for j in range(sums.shape[0]):
        sums[j] = before_sums[j]
    for at, (x_ref, (step, odd, other)) in enumerate(zip(x_refs, x_kinds)):
        valid, first_inner = inner_of(n_col, nb_rows, nb_cols, chain_tile(c, step, odd), 1 - l if other else l)
        n_slots = jnp.where(valid, places[at, SLOTS], 0)
        list_pairs(todo, 0, places, at, n_slots, first_inner, slots_of, n_of, nb_rows, nb_cols)
        multiply_pairs(todo, 0, x_ref, y_blocks, acc, sums)
    if is_last:
        totals = refs[3]
        totals[...] = jnp.zeros(totals.shape, totals.dtype)
        for j in range(nb_cols):
            totals[j : j + 1, :] = jnp.sum(sums[j], axis=0, keepdims=True)


def multiply_late(place, slots_of, n_of, y_blocks, xs, x_kinds, acc, sums, is_last, n_col, nb_rows, nb_cols):
    totals = jax.ShapeDtypeStruct((8, BLK), jnp.float32)
    same_sums = jax.ShapeDtypeStruct(sums.shape, sums.dtype)
    operands = [place, slots_of, n_of, y_blocks, *xs, acc, sums]
    return pl.pallas_call(
        functools.partial(late_kernel, n_col, nb_rows, nb_cols, x_kinds, is_last),
        out_shape=[jax.ShapeDtypeStruct(acc.shape, acc.dtype), totals if is_last else same_sums],
        in_specs=[SMEM] * 3 + [VMEM] * (len(operands) - 3),
        out_specs=[VMEM, VMEM],
        input_output_aliases={len(operands) - 2: 0},
        scratch_shapes=([pltpu.VMEM(sums.shape, jnp.float32)] if is_last else [])
        + list_scratch(0, nb_rows, nb_cols, len(xs))[2:],
        compiler_params=pltpu.CompilerParams(vmem_limit_bytes=8 * MIB),
        cost_estimate=SMALL,
        name="multiply_last" if is_last else "multiply_late",
    )(*operands)


def scale_kernel(scaling, nb_rows, nb_cols, *refs):
    product, sums = refs[0], refs[1:-3]
    out, scaled, sems = refs[-3:]
    total = sums[0][...]
    for other in sums[1:]:
        total = total + other[...]
    factor = scaling / total[0:nb_cols, :]

    def out_copy(i):
        rows = pl.ds(pl.multiple_of(i * BLK, BLK), BLK)
        return pltpu.make_async_copy(scaled.at[rows, :], out.at[rows, :], sems.at[i])

    def square(i, carry):
        for j in range(nb_cols):
            value = product[i * nb_cols + j]
            scaled[pl.ds(pl.multiple_of(i * BLK, BLK), BLK), j * BLK : (j + 1) * BLK] = (
                value * value * factor[j : j + 1, :]
            )
        out_copy(i).start()
        return carry

    lax.fori_loop(0, nb_rows, square, 0)

    def wait(i, carry):
        out_copy(i).wait()
        return carry

    lax.fori_loop(0, nb_rows, wait, 0)


def scale(product, sums, scaling, nb_rows, nb_cols):
    shape = (nb_rows * BLK, nb_cols * BLK)
    return pl.pallas_call(
        functools.partial(scale_kernel, scaling, nb_rows, nb_cols),
        out_shape=jax.ShapeDtypeStruct(shape, jnp.float32),
        in_specs=[VMEM] * (1 + len(sums)),
        out_specs=ANY,
        scratch_shapes=[pltpu.VMEM(shape, jnp.float32), pltpu.SemaphoreType.DMA((nb_rows,))],
        compiler_params=pltpu.CompilerParams(vmem_limit_bytes=8 * MIB),
        cost_estimate=pl.CostEstimate(flops=10**7, bytes_accessed=10 * 10**6, transcendentals=0),
        name="scale",
    )(product, *sums)


def even_tile(i, step):
    return i + step if i % 2 == 0 else i - step


def odd_tile(i, step):
    return i - step if i % 2 == 0 else i + step


def body(n_row, n_col, similarity, block_mask):
    nb_rows, nb_cols = block_mask.shape
    r, c, l = lax.axis_index("row"), lax.axis_index("col"), lax.axis_index("layer")
    place = jnp.stack([r, c, l]).astype(jnp.int32)
    mask = block_mask.T

    def hop(x, tile):
        pairs = []
        for i in range(n_col):
            partner = tile(i, 1)
            for layer in range(2):
                if 0 <= partner < n_col:
                    pairs.append((2 * i + layer, 2 * partner + layer))
                else:
                    pairs.append((2 * i + layer, 2 * i + 1 - layer))
        return lax.ppermute(x, ("col", "layer"), pairs)

    def sibling(x):
        return lax.ppermute(x, "layer", [(0, 1), (1, 0)])

    own = compact(mask, similarity)
    even = hop(own, even_tile)
    odd = hop(own, odd_tile)
    near = [m for m in range(n_row) if m.bit_count() <= 1]
    ys = [own] + [None] * (n_row - 1)
    for m in near[1:]:
        ys[m] = lax.ppermute(own, "row", [(s, s ^ m) for s in range(n_row)])
    for m in range(1, n_row):
        if ys[m] is None:
            bit = 1 << (m.bit_length() - 1)
            ys[m] = lax.ppermute(ys[m ^ bit], "row", [(s, s ^ bit) for s in range(n_row)])
    first_xs = [sibling(own), odd, even]
    shares = [((0, False, True, True), first_xs[0]), ((1, True, False, True), odd), ((1, False, False, True), even)]
    acc, sums, y_blocks = multiply_first(place, near, ys, first_xs, n_row, n_col, nb_rows, nb_cols)
    for step in range(1, n_col - 2):
        shares.append(((step, True, True, False), sibling(odd)))
        shares.append(((step, False, True, False), sibling(even)))
        odd, even = hop(even, odd_tile), hop(odd, even_tile)
        shares += [((step + 1, True, False, False), odd), ((step + 1, False, False, False), even)]
    odd, sums = lax.optimization_barrier((odd, sums))
    last = hop(odd, even_tile)
    arrived = jnp.where(jnp.logical_or(c == 0, c == n_col - 1), even, odd)
    halves = [sibling(arrived[:FIRST_ROWS]), sibling(arrived[FIRST_ROWS:])]
    x_kinds, xs = zip(*shares)
    acc, sums, y_blocks, slots_of, n_of = multiply_second(
        place, near, ys, xs, x_kinds, halves, acc, sums, y_blocks, n_col, nb_rows, nb_cols
    )
    last, sums = lax.optimization_barrier((last, sums))
    other = sibling(last)
    kinds = [(n_col - 1, False, False)]
    sizes = n_col, nb_rows, nb_cols
    acc, sums = multiply_late(place, slots_of, n_of, y_blocks, [last], kinds, acc, sums, False, *sizes)
    kinds = [(n_col - 1, False, True)]
    product, sums = multiply_late(place, slots_of, n_of, y_blocks, [other], kinds, acc, sums, True, *sizes)
    all_sums = [sums]
    for m in range(1, n_row):
        all_sums.append(lax.ppermute(sums, "row", [(s, s ^ m) for s in range(n_row)]))
    return scale(product, all_sums, float(nb_rows * BLK * n_row), nb_rows, nb_cols)


def solution(mesh):
    n_row, n_col = mesh.shape["row"], mesh.shape["col"]
    return jax.shard_map(
        functools.partial(body, n_row, n_col),
        mesh=mesh,
        in_specs=(P("row", ("col", "layer")), P("row", ("col", "layer"))),
        out_specs=P("row", ("col", "layer")),
        check_vma=False,
    )
```

```python
import functools

import jax
import jax.numpy as jnp
from jax import lax
from jax.experimental import pallas as pl
from jax.experimental.pallas import tpu as pltpu
from jax.sharding import PartitionSpec as P

BLK = 128
SLOTS = 18
SHARE = SLOTS * BLK
HEAD = 16
HALF = 9
PIECE = 64
ROWS = HEAD + SHARE
FIRST_ROWS = HEAD + HALF * BLK
UNROLL = 8
LAG = 3
MIB = 1024 * 1024

SMEM = pl.BlockSpec(memory_space=pltpu.SMEM)
VMEM = pl.BlockSpec(memory_space=pltpu.VMEM)
ANY = pl.BlockSpec(memory_space=pl.ANY)
SMALL = pl.CostEstimate(flops=10**8, bytes_accessed=10**6, transcendentals=0)


def compact_kernel(mask_ref, sim_ref, out_ref, places, sems):
    nb_cols, nb_rows = mask_ref.shape

    def block_copy(slot, i, k):
        block = sim_ref.at[pl.ds(pl.multiple_of(i * BLK, BLK), BLK), pl.ds(k * BLK, BLK)]
        return pltpu.make_async_copy(
            block, out_ref.at[pl.ds(pl.multiple_of(HEAD + slot * BLK, HEAD), BLK), :], sems.at[slot]
        )

    def scan(i, count):
        for k in range(nb_cols):
            here = mask_ref[k, i]

            @pl.when(here != 0)
            def _():
                block_copy(count, i, k).start()
                places[count] = i * 8 + k

            count = count + here
        return count

    for slot in range(SLOTS):
        places[slot] = 0
    count = lax.fori_loop(0, nb_rows, scan, jnp.int32(0))
    lane = lax.broadcasted_iota(jnp.int32, (HEAD, BLK), 1)
    header = jnp.where(lane == SLOTS, count, 0)
    for slot in range(SLOTS):
        header = jnp.where(lane == slot, places[slot], header)
    out_ref[0:HEAD, :] = header.astype(jnp.float32).astype(out_ref.dtype)

    def wait(slot, carry):
        block_copy(slot, 0, 0).wait()
        return carry

    lax.fori_loop(0, count, wait, 0)


def compact(mask, similarity):
    return pl.pallas_call(
        compact_kernel,
        out_shape=pltpu.VMEM((ROWS, BLK), similarity.dtype),
        in_specs=[SMEM, ANY],
        out_specs=VMEM,
        scratch_shapes=[pltpu.SMEM((SLOTS,), jnp.int32), pltpu.SemaphoreType.DMA((SLOTS,))],
        cost_estimate=pl.CostEstimate(flops=0, bytes_accessed=2 * SHARE * BLK * 2, transcendentals=0),
        name="compact",
    )(mask, similarity)


def multiply_pairs(todo, share, x_ref, y_blocks, acc, sums, x_base=0):
    def multiply(step, carry):
        terms = []

        def add_term(packed, term):
            at = jnp.bitwise_and(packed, 127)
            j = jnp.bitwise_and(lax.shift_right_logical(packed, 19), 7)
            old = acc[at]
            new = old + term
            acc[at] = new
            sums[j] += jnp.sum((term * (old + new)).reshape(BLK // 8, 8, BLK), axis=0)

        for u in range(UNROLL):
            packed = todo[share, 1 + step * UNROLL + u]
            x = x_base + HEAD + lax.shift_right_logical(packed, 22) * BLK
            y = jnp.bitwise_and(lax.shift_right_logical(packed, 7), 4095) * HEAD
            x_block = x_ref[pl.ds(pl.multiple_of(x, HEAD), BLK), :]
            y_block = y_blocks[pl.ds(pl.multiple_of(y, HEAD), BLK), :]
            terms.append((packed, jnp.dot(x_block, y_block, preferred_element_type=jnp.float32)))
            if u >= LAG:
                add_term(*terms[u - LAG])
        for packed, term in terms[UNROLL - LAG :]:
            add_term(packed, term)
        return carry

    n_steps = lax.shift_right_logical(todo[share, 0] + UNROLL - 1, UNROLL.bit_length() - 1)
    lax.fori_loop(0, n_steps, multiply, 0)


def list_pairs(todo, share, places, at, n_slots, first_inner, slots_of, n_of, nb_rows, nb_cols, first_slot=0):
    def slot_pairs(slot, count):
        place = places[at, slot]
        k = first_inner + jnp.bitwise_and(place, 7)
        packed = (slot << 22) + lax.shift_right_logical(place, 3) * nb_cols

        n_pairs = n_of[k]

        def pair(n, carry):
            todo[share, 1 + count + n] = packed + slots_of[k * 8 + n]
            return carry

        pair(0, 0)
        pair(1, 0)
        lax.fori_loop(2, n_pairs, pair, 0)
        return count + n_pairs

    count = lax.fori_loop(first_slot, n_slots, slot_pairs, jnp.int32(0))
    for u in range(UNROLL):
        todo[share, 1 + count + u] = (first_slot << 22) + (nb_cols << 19) + nb_rows * nb_cols
    todo[share, 0] = count


def clear_blocks(ref):
    def clear(at, carry):
        ref[at] = jnp.zeros(ref.shape[1:], ref.dtype)
        return carry

    lax.fori_loop(0, ref.shape[0], clear, 0)


def read_headers(headers, heads, places):
    for at, header in enumerate(headers):
        heads[at : at + 1, :] = header.astype(jnp.float32)[0:1, :].astype(jnp.int32)
    for at in range(len(headers)):
        for slot in range(SLOTS + 1):
            places[at, slot] = heads[at, slot]


def inner_of(n_col, nb_rows, nb_cols, tile, layer):
    valid = jnp.logical_and(tile >= 0, tile < n_col)
    return valid, jnp.where(valid, tile, 0) * nb_rows + layer * nb_cols


def tile_rows(y_blocks, tile, rows=ROWS):
    return y_blocks.at[pl.ds(pl.multiple_of(tile * ROWS, HEAD), rows), :]


def column_headers(y_blocks, r, n_row):
    return [tile_rows(y_blocks, jnp.bitwise_xor(r, m), HEAD)[...] for m in range(n_row)]


def list_column(slots_of, n_of, places, sources, r, nb_rows):
    def no_slots(k, carry):
        n_of[k] = 0
        return carry

    lax.fori_loop(0, n_of.shape[0], no_slots, 0)
    for at, m in sources:
        tile = jnp.bitwise_xor(r, m)
        first = tile * (ROWS // HEAD) + 1

        def put(slot, carry):
            place = places[at, slot]
            k = tile * nb_rows + lax.shift_right_logical(place, 3)
            n = n_of[k]
            j = jnp.bitwise_and(place, 7)
            slots_of[k * 8 + n] = (j << 19) + ((first + slot * (BLK // HEAD)) << 7) + j
            n_of[k] = n + 1
            return carry

        lax.fori_loop(0, places[at, SLOTS], put, 0)


def chain_tile(c, step, odd):
    forward = 1 - 2 * jnp.bitwise_and(c, 1)
    return c - step * forward if odd else c + step * forward


def first_kernel(near, n_col, nb_rows, nb_cols, place_ref, *refs):
    own_ref, refs = refs[0], refs[1:]
    y_refs, refs = refs[: len(near) - 1], refs[len(near) - 1 :]
    x_refs, refs = refs[:2], refs[2:]
    acc, sums, y_blocks, slots_of, n_of, own_head, heads, places, todo, y_sems = refs
    r, c, l = place_ref[0], place_ref[1], place_ref[2]
    head_copy = pltpu.make_async_copy(own_ref.at[pl.ds(0, HEAD), :], own_head, y_sems.at[len(near)])
    head_copy.start()
    copies = []
    for at, (m, y_ref) in enumerate(zip(near, (own_ref, *y_refs))):
        copies.append(pltpu.make_async_copy(y_ref, tile_rows(y_blocks, jnp.bitwise_xor(r, m)), y_sems.at[at]))
        copies[-1].start()
    head_copy.wait()
    headers = [own_head[...]] + [ref[0:HEAD, :] for ref in (*y_refs, *x_refs)]
    read_headers(headers, heads, places)
    clear_blocks(acc)
    clear_blocks(sums)
    list_column(slots_of, n_of, places, list(enumerate(near)), r, nb_rows)
    for copy in copies:
        copy.wait()
    shares = [(c, l, 0, y_blocks, r * ROWS), (c, 1 - l, len(near), x_refs[0], 0)]
    shares.append((chain_tile(c, 1, False), l, len(near) + 1, x_refs[1], 0))
    for tile, layer, at, x_ref, x_base in shares:
        valid, first_inner = inner_of(n_col, nb_rows, nb_cols, tile, layer)
        n_slots = jnp.where(valid, places[at, SLOTS], 0)
        list_pairs(todo, 0, places, at, n_slots, first_inner, slots_of, n_of, nb_rows, nb_cols)
        multiply_pairs(todo, 0, x_ref, y_blocks, acc, sums, x_base)


def list_scratch(n_row, nb_rows, nb_cols, shares):
    return [
        pltpu.SMEM((n_row * nb_rows * 8,), jnp.int32),
        pltpu.SMEM((n_row * nb_rows,), jnp.int32),
        pltpu.VMEM((shares, BLK), jnp.int32),
        pltpu.SMEM((shares, BLK), jnp.int32),
        pltpu.SMEM((1, SLOTS * nb_cols + 1 + UNROLL), jnp.int32),
    ]


def multiply_first(place, near, ys, xs, n_row, n_col, nb_rows, nb_cols):
    shares = len(near) + len(xs)
    lists = list_scratch(n_row, nb_rows, nb_cols, shares)
    return pl.pallas_call(
        functools.partial(first_kernel, near, n_col, nb_rows, nb_cols),
        out_shape=[
            jax.ShapeDtypeStruct((nb_rows * nb_cols + 1, BLK, BLK), jnp.float32),
            jax.ShapeDtypeStruct((nb_cols + 1, 8, BLK), jnp.float32),
            jax.ShapeDtypeStruct((n_row * ROWS, BLK), jnp.bfloat16),
        ],
        in_specs=[SMEM, ANY] + [VMEM] * (shares - 1),
        out_specs=[VMEM] * 3,
        scratch_shapes=lists[:2]
        + [pltpu.VMEM((HEAD, BLK), jnp.bfloat16)]
        + lists[2:]
        + [pltpu.SemaphoreType.DMA((len(near) + 1,))],
        compiler_params=pltpu.CompilerParams(vmem_limit_bytes=24 * MIB),
        cost_estimate=SMALL,
        name="multiply_first",
    )(place, *[ys[m] for m in near], *xs)


def second_kernel(near, n_row, n_col, nb_rows, nb_cols, x_kinds, place_ref, *refs):
    distant = [m for m in range(n_row) if m not in near]
    y_refs, refs = refs[: len(distant)], refs[len(distant) :]
    x_refs, refs = refs[: len(x_kinds)], refs[len(x_kinds) :]
    half_refs, refs = refs[:2], refs[2:]
    acc, sums, y_blocks, slots_of, n_of, heads, places, todo, y_sems = refs[3:]
    r, c, l = place_ref[0], place_ref[1], place_ref[2]
    copies = []
    for at, (m, y_ref) in enumerate(zip(distant, y_refs)):
        copies.append(pltpu.make_async_copy(y_ref, tile_rows(y_blocks, jnp.bitwise_xor(r, m)), y_sems.at[at]))
        copies[-1].start()
    for copy in copies:
        copy.wait()
    headers = column_headers(y_blocks, r, n_row) + [ref[0:HEAD, :] for ref in (*x_refs, half_refs[0])]
    read_headers(headers, heads, places)
    list_column(slots_of, n_of, places, [(m, m) for m in range(n_row)], r, nb_rows)
    shares = [((0, False, False, True), 0, y_blocks, r * ROWS)]
    shares += [(kind, n_row + at, x_ref, 0) for at, (kind, x_ref) in enumerate(zip(x_kinds, x_refs))]
    for (step, odd, other, rest), at, x_ref, x_base in shares:
        tile = chain_tile(c, step, odd)
        valid, first_inner = inner_of(n_col, nb_rows, nb_cols, tile, 1 - l if other else l)
        if rest:
            for m in near:
                valid = jnp.logical_and(valid, jnp.bitwise_xor(tile, r) != m)
        n_slots = jnp.where(valid, places[at, SLOTS], 0)
        list_pairs(todo, 0, places, at, n_slots, first_inner, slots_of, n_of, nb_rows, nb_cols)
        multiply_pairs(todo, 0, x_ref, y_blocks, acc, sums, x_base)
    is_end = jnp.logical_or(c == 0, c == n_col - 1)
    step, at = n_col - 2, n_row + len(x_refs)
    tile = jnp.where(is_end, chain_tile(c, step, False), chain_tile(c, step, True))
    valid, first_inner = inner_of(n_col, nb_rows, nb_cols, tile, 1 - l)
    n_slots = jnp.where(valid, places[at, SLOTS], 0)
    for first_slot, end, x_ref, x_base in (
        (0, jnp.minimum(n_slots, HALF), half_refs[0], 0),
        (HALF, n_slots, half_refs[1], -FIRST_ROWS),
    ):
        list_pairs(todo, 0, places, at, end, first_inner, slots_of, n_of, nb_rows, nb_cols, first_slot)
        multiply_pairs(todo, 0, x_ref, y_blocks, acc, sums, x_base)


def multiply_second(place, near, ys, xs, x_kinds, halves, acc, sums, y_blocks, n_col, nb_rows, nb_cols):
    n_row = len(ys)
    distant = [ys[m] for m in range(n_row) if m not in near]
    operands = [place, *distant, *xs, *halves, acc, sums, y_blocks]
    lists = list_scratch(n_row, nb_rows, nb_cols, n_row + len(xs) + 1)
    return pl.pallas_call(
        functools.partial(second_kernel, near, n_row, n_col, nb_rows, nb_cols, x_kinds),
        out_shape=[jax.ShapeDtypeStruct(x.shape, x.dtype) for x in (acc, sums, y_blocks)]
        + [jax.ShapeDtypeStruct(x.shape, x.dtype) for x in lists[:2]],
        in_specs=[SMEM] + [ANY] * len(distant) + [VMEM] * (len(xs) + 5),
        out_specs=[VMEM] * 3 + [SMEM] * 2,
        input_output_aliases={len(operands) - 3 + at: at for at in range(3)},
        scratch_shapes=lists[2:] + [pltpu.SemaphoreType.DMA((len(distant),))],
        compiler_params=pltpu.CompilerParams(vmem_limit_bytes=24 * MIB),
        cost_estimate=SMALL,
        name="multiply_second",
    )(*operands)


def late_kernel(n_col, nb_rows, nb_cols, x_kinds, is_last, place_ref, slots_of, n_of, y_blocks, *refs):
    x_refs, refs = refs[: len(x_kinds)], refs[len(x_kinds) :]
    _, before_sums, acc = refs[:3]
    sums, heads, places, todo = refs[-4:]
    c, l = place_ref[1], place_ref[2]
    read_headers([ref[0:HEAD, :] for ref in x_refs], heads, places)
    for j in range(sums.shape[0]):
        sums[j] = before_sums[j]
    for at, (x_ref, (step, odd, other)) in enumerate(zip(x_refs, x_kinds)):
        valid, first_inner = inner_of(n_col, nb_rows, nb_cols, chain_tile(c, step, odd), 1 - l if other else l)
        n_slots = jnp.where(valid, places[at, SLOTS], 0)
        list_pairs(todo, 0, places, at, n_slots, first_inner, slots_of, n_of, nb_rows, nb_cols)
        multiply_pairs(todo, 0, x_ref, y_blocks, acc, sums)
    if is_last:
        totals = refs[3]
        totals[...] = jnp.zeros(totals.shape, totals.dtype)
        for j in range(nb_cols):
            totals[j : j + 1, :] = jnp.sum(sums[j], axis=0, keepdims=True)


def multiply_late(place, slots_of, n_of, y_blocks, xs, x_kinds, acc, sums, is_last, n_col, nb_rows, nb_cols):
    totals = jax.ShapeDtypeStruct((8, BLK), jnp.float32)
    same_sums = jax.ShapeDtypeStruct(sums.shape, sums.dtype)
    operands = [place, slots_of, n_of, y_blocks, *xs, acc, sums]
    return pl.pallas_call(
        functools.partial(late_kernel, n_col, nb_rows, nb_cols, x_kinds, is_last),
        out_shape=[jax.ShapeDtypeStruct(acc.shape, acc.dtype), totals if is_last else same_sums],
        in_specs=[SMEM] * 3 + [VMEM] * (len(operands) - 3),
        out_specs=[VMEM, VMEM],
        input_output_aliases={len(operands) - 2: 0},
        scratch_shapes=([pltpu.VMEM(sums.shape, jnp.float32)] if is_last else [])
        + list_scratch(0, nb_rows, nb_cols, len(xs))[2:],
        compiler_params=pltpu.CompilerParams(vmem_limit_bytes=24 * MIB),
        cost_estimate=SMALL,
        name="multiply_last" if is_last else "multiply_late",
    )(*operands)


def scale_kernel(scaling, nb_rows, nb_cols, *refs):
    product, sums = refs[0], refs[1:-3]
    out, scaled, sems = refs[-3:]
    total = sums[0][...]
    for other in sums[1:]:
        total = total + other[...]
    factor = scaling / total[0:nb_cols, :]

    def out_copy(i):
        rows = pl.ds(pl.multiple_of(i * PIECE, PIECE), PIECE)
        return pltpu.make_async_copy(scaled.at[rows, :], out.at[rows, :], sems.at[i])

    def square(i, carry):
        for part in range(BLK // PIECE):
            for j in range(nb_cols):
                value = product[i * nb_cols + j, part * PIECE : (part + 1) * PIECE, :]
                rows = pl.ds(pl.multiple_of(i * BLK + part * PIECE, PIECE), PIECE)
                scaled[rows, j * BLK : (j + 1) * BLK] = value * value * factor[j : j + 1, :]
            out_copy(i * (BLK // PIECE) + part).start()
        return carry

    lax.fori_loop(0, nb_rows, square, 0)

    def wait(i, carry):
        out_copy(i).wait()
        return carry

    lax.fori_loop(0, nb_rows * (BLK // PIECE), wait, 0)


def scale(product, sums, scaling, nb_rows, nb_cols):
    shape = (nb_rows * BLK, nb_cols * BLK)
    return pl.pallas_call(
        functools.partial(scale_kernel, scaling, nb_rows, nb_cols),
        out_shape=jax.ShapeDtypeStruct(shape, jnp.float32),
        in_specs=[VMEM] * (1 + len(sums)),
        out_specs=ANY,
        scratch_shapes=[pltpu.VMEM(shape, jnp.float32), pltpu.SemaphoreType.DMA((nb_rows * (BLK // PIECE),))],
        compiler_params=pltpu.CompilerParams(vmem_limit_bytes=16 * MIB),
        cost_estimate=pl.CostEstimate(flops=10**7, bytes_accessed=10 * 10**6, transcendentals=0),
        name="scale",
    )(product, *sums)


def even_tile(i, step):
    return i + step if i % 2 == 0 else i - step


def odd_tile(i, step):
    return i - step if i % 2 == 0 else i + step


def body(n_row, n_col, similarity, block_mask):
    nb_rows, nb_cols = block_mask.shape
    r, c, l = lax.axis_index("row"), lax.axis_index("col"), lax.axis_index("layer")
    place = jnp.stack([r, c, l]).astype(jnp.int32)
    mask = block_mask.T

    def hop(x, tile):
        pairs = []
        for i in range(n_col):
            partner = tile(i, 1)
            for layer in range(2):
                if 0 <= partner < n_col:
                    pairs.append((2 * i + layer, 2 * partner + layer))
                else:
                    pairs.append((2 * i + layer, 2 * i + 1 - layer))
        return lax.ppermute(x, ("col", "layer"), pairs)

    def sibling(x):
        return lax.ppermute(x, "layer", [(0, 1), (1, 0)])

    own = compact(mask, similarity)
    even = hop(own, even_tile)
    odd = hop(own, odd_tile)
    near = [m for m in range(n_row) if m.bit_count() <= 1]
    ys = [own] + [None] * (n_row - 1)
    for m in near[1:]:
        ys[m] = lax.ppermute(own, "row", [(s, s ^ m) for s in range(n_row)])
    for m in range(1, n_row):
        if ys[m] is None:
            bit = 1 << (m.bit_length() - 1)
            ys[m] = lax.ppermute(ys[m ^ bit], "row", [(s, s ^ bit) for s in range(n_row)])
    first_xs = [sibling(own), even]
    shares = [((0, False, True, True), first_xs[0]), ((1, True, False, False), odd), ((1, False, False, True), even)]
    first_xs[1], _ = lax.optimization_barrier((even, odd))
    acc, sums, y_blocks = multiply_first(place, near, ys, first_xs, n_row, n_col, nb_rows, nb_cols)
    for step in range(1, n_col - 2):
        shares.append(((step, True, True, False), sibling(odd)))
        shares.append(((step, False, True, False), sibling(even)))
        odd, even = hop(even, odd_tile), hop(odd, even_tile)
        shares += [((step + 1, True, False, False), odd), ((step + 1, False, False, False), even)]
    odd, sums = lax.optimization_barrier((odd, sums))
    last = hop(odd, even_tile)
    arrived = jnp.where(jnp.logical_or(c == 0, c == n_col - 1), even, odd)
    halves = [sibling(arrived[:FIRST_ROWS]), sibling(arrived[FIRST_ROWS:])]
    x_kinds, xs = zip(*shares)
    acc, sums, y_blocks, slots_of, n_of = multiply_second(
        place, near, ys, xs, x_kinds, halves, acc, sums, y_blocks, n_col, nb_rows, nb_cols
    )
    last, sums = lax.optimization_barrier((last, sums))
    other = sibling(last)
    kinds = [(n_col - 1, False, False)]
    sizes = n_col, nb_rows, nb_cols
    acc, sums = multiply_late(place, slots_of, n_of, y_blocks, [last], kinds, acc, sums, False, *sizes)
    kinds = [(n_col - 1, False, True)]
    product, sums = multiply_late(place, slots_of, n_of, y_blocks, [other], kinds, acc, sums, True, *sizes)
    all_sums = [sums]
    for m in range(1, n_row):
        all_sums.append(lax.ppermute(sums, "row", [(s, s ^ m) for s in range(n_row)]))
    return scale(product, all_sums, float(nb_rows * BLK * n_row), nb_rows, nb_cols)


def solution(mesh):
    n_row, n_col = mesh.shape["row"], mesh.shape["col"]
    return jax.shard_map(
        functools.partial(body, n_row, n_col),
        mesh=mesh,
        in_specs=(P("row", ("col", "layer")), P("row", ("col", "layer"))),
        out_specs=P("row", ("col", "layer")),
        check_vma=False,
    )
```
